32 devices in a mesh: groups: 2 (over y), store: 4 (over z), tensor: 4 (over x, core).
Axes of the slice: x: 2, y: 2, z: 4, core: 2. Of those that a mesh axis runs over, the one named last changes fastest.
Arguments:
- normed_input: bfloat16 [2, 128, 8192], P(None, ('groups', 'store'), 'tensor'), parts along dimension 1, may hold values from -6 to 6
- kv_weight: bfloat16 [2, 8192, 2048], P(None, 'tensor'), may hold values from -0.0625 to 0.0625
- down_adapters: bfloat16 [2, 128, 8192, 64], P(None, 'store', 'tensor'), may hold values from -0.0625 to 0.0625
- up_adapters: bfloat16 [2, 128, 64, 2048], P(None, 'store', None, 'tensor'), may hold values from -0.75 to 0.75
- request_owner: int32 [128, 1], P(('groups', 'store')), parts along dimension 0, may hold values from 0 to 3; in each aligned block of 16 rows (0 to 15, 16 to 31, ...) at most 4 rows name the same one
- request_slot: int32 [128], P(('groups', 'store')), parts along dimension 0, may hold values from 0 to 31
- request_count: int32 [8], P(('groups', 'store')), parts along dimension 0, may hold values from 8 to 16, as said below
Outputs:
- key_values: bfloat16 [2, 128, 2048], P(None, ('groups', 'store'), 'tensor'), parts along dimension 1
The draws below stay inside these ranges and needn't reach their ends.
There are 2 independent parts, one for each index of `groups`. The reference program is written for one: setup_inputs(seed, part) draws one part's arguments, and reference() takes and returns one part's arrays. A program takes and returns all parts, laid end to end along the dimension named above; an argument that names none is the same for every part. Nothing has to cross between parts.
Inputs may be any that keep to these rules, and one draw needn't show every extreme that they name: `request_owner`: among the 16 rows of one store shard, at most 4 name the same owner shard. Slots of shard s at index request_count[s] or later are unused; some shard is full.
All inputs are finite; a program needn't handle non-finite values.
Results may differ from the reference program's by a relative error of at most 0.0042.
Values may be sent and summed in bfloat16 or wider, within the bound.
No kernel may reach another device: no remote copies, remote signals or barrier semaphores. Data moves between devices by JAX's collectives and lax.ppermute only.
A program may use at most 128 MiB of HBM per device.

```python
import math
import jax
import jax.numpy as jnp
import numpy as np
from jax import lax

D = 8192
KV = 2048
R = 64
LAYERS = 2
REQ_DEV = 16
ADP_DEV = 32
CAP = 4
TOKENS = 64
ADAPTERS = 128
N_STORE = 4


def draw_request_count(key, part):
    key = jax.random.fold_in(key, 7)
    first_key, second_key = jax.random.split(key)
    counts = jax.random.randint(first_key, (N_STORE,), REQ_DEV // 2, REQ_DEV + 1)
    full_shard = jax.random.randint(second_key, (), 0, N_STORE)
    return jnp.where(jnp.arange(N_STORE) == full_shard, REQ_DEV, counts).astype(jnp.int32)


def with_ends(values, key, least, largest):
    longest = values.shape.index(max(values.shape))
    spots = []
    for shift in (0, 1):
        where = [jax.random.randint(jax.random.fold_in(key, axis), (), 0, length) for axis, length in enumerate(values.shape)]
        where[longest] = (where[longest] + shift) % values.shape[longest]
        spots.append(tuple(where))
    return values.at[spots[0]].set(least).at[spots[1]].set(largest)


def block_scale(stream_key, dims, cuts, least, high):
    factor_of, own = 1.0, jax.random.fold_in(stream_key, 6)
    for axis_at, blocks in cuts:
        draws = jnp.exp(jax.random.uniform(jax.random.fold_in(own, axis_at), (blocks,), jnp.float32, least / len(cuts), high / len(cuts)))
        factor_of = factor_of * jnp.repeat(draws, dims[axis_at] // blocks).reshape([-1 if axis == axis_at else 1 for axis in range(len(dims))])
    return factor_of


def shared_out(own_key, own, number, rows, amount, top, bound, lean):
    order = jax.random.permutation(own_key, amount)
    packed, usual = shares(amount, rows * top, bound, lean, True), shares(amount, rows * top, bound, lean, False)
    places = jnp.arange(amount)

    def named(lengths, rotation):
        used = int((lengths > 0).sum())
        fixed = max(1, used // 4)
        moved = fixed + (places - fixed + rotation * (used - fixed)) % max(1, amount - fixed)
        return jnp.zeros((amount,), jnp.int32).at[order[jnp.where(places < fixed, places, moved)]].set(jnp.asarray(lengths, jnp.int32))

    lengths = jnp.where(number % 4 == 0, named(packed, number // 4), named(usual, number - number // 4 - 1))
    mixed = jax.random.permutation(jax.random.fold_in(own, 3), amount)
    donor, sink = mixed[0:amount // 2 * 2:2], mixed[1:amount // 2 * 2:2]
    slack = jnp.minimum(lengths[donor] - 1, bound - lengths[sink]) // 2
    slack = jnp.where((donor == order[0]) | (sink == order[0]) | (lengths[sink] == 0), 0, jnp.maximum(slack, 0))
    moved = jax.random.randint(jax.random.fold_in(own, 4), (amount // 2,), 0, 1 << 20) % (slack + 1)
    lengths = lengths.at[donor].add(-moved).at[sink].add(moved)
    labels = jnp.searchsorted(jnp.cumsum(lengths), jnp.arange(rows * top), side="right").astype(jnp.int32)
    table = labels.reshape(top, rows).T
    table = table[jax.random.permutation(jax.random.fold_in(own, 1), rows)]
    rotation = jax.random.randint(jax.random.fold_in(own, 2), (rows, 1), 0, top)
    return jnp.take_along_axis(table, (jnp.arange(top)[None, :] + rotation) % top, axis=1)


def shares(count, total, most, skew, full):
    loads = [(1 << 20) // math.isqrt(grade ** skew) + 1 for grade in range(1, count + 1)]
    largest = most if full else min(most, max(-(-total // count), total * loads[0] // sum(loads)))
    least = 1 if total - largest >= count - 1 else 0
    given, spare = [largest] + [least] * (count - 1), total - largest - least * (count - 1)
    while spare > 0:
        free = [i for i in range(1, count) if given[i] < largest] or [i for i in range(1, count) if given[i] < most]
        mass, remaining = sum([loads[i] for i in free]), spare
        for i in free:
            extra = min(most - given[i], max(1, remaining * loads[i] // mass), spare)
            given[i] = given[i] + extra
            spare = spare - extra
    return np.array(given)


def noise(own_key, extent, width, reach, cuts=(), kind=jnp.bfloat16):
    factor_of = block_scale(own_key, extent, cuts, -0.22, 0.18) if cuts else 1.0
    array = jax.random.normal(own_key, extent, jnp.float32) * width * factor_of
    return jnp.minimum(jnp.maximum(array, -reach), reach).astype(kind)


def setup_inputs(seed: int = 0, part: int = 0) -> dict:
    splits = jax.random.split(jax.random.key(seed), 8)
    own_keys = jax.random.split(jax.random.fold_in(splits[7], part), 8)
    normed_input = noise(own_keys[0], (LAYERS, TOKENS, D), 1.0, 6.0, ((1, 4), (2, 4)))
    kv_weight = noise(splits[1], (LAYERS, D, KV), D ** -0.5, 0.0625, ((1, 4),))
    down_adapters = noise(splits[2], (LAYERS, ADAPTERS, D, R), D ** -0.5, 0.0625, ((1, 4), (2, 4)))
    up_adapters = noise(splits[3], (LAYERS, ADAPTERS, R, KV), R ** -0.5, 0.75, ((1, 4), (3, 4)))
    request_owner_keys = jax.random.split(jax.random.fold_in(own_keys[4], 1), TOKENS // REQ_DEV)
    request_owner_turns = jax.random.permutation(jax.random.fold_in(own_keys[4], 3), TOKENS // REQ_DEV)
    request_owner = jax.vmap(lambda own, number: shared_out(jax.random.fold_in(own_keys[4], 2), own, number, REQ_DEV, N_STORE, 1, CAP, 2))(request_owner_keys, request_owner_turns).reshape((TOKENS, 1))
    request_slot = with_ends(jax.random.randint(own_keys[5], (TOKENS,), 0, ADP_DEV), jax.random.fold_in(own_keys[5], 1), 0, ADP_DEV - 1).astype(jnp.int32)
    request_count = draw_request_count(jax.random.fold_in(jax.random.fold_in(splits[7], part), 71), part)
    return dict(normed_input=normed_input, kv_weight=kv_weight, down_adapters=down_adapters, up_adapters=up_adapters, request_owner=request_owner, request_slot=request_slot, request_count=request_count)


def reference(normed_input, kv_weight, down_adapters, up_adapters, request_owner, request_slot, request_count):
    adapter_ids = (request_owner[:, 0] * ADP_DEV + request_slot).astype(jnp.int32)
    slot_index = jnp.arange(TOKENS, dtype=jnp.int32)
    shard_index = slot_index // REQ_DEV
    live_rows = (slot_index - shard_index * REQ_DEV) < request_count[shard_index]
    results = []
    for layer_index in range(LAYERS):
        rows_in = normed_input[layer_index]
        base_part = jnp.dot(rows_in, kv_weight[layer_index], preferred_element_type=jnp.float32)
        down_layer = down_adapters[layer_index]
        up_layer = up_adapters[layer_index]

        def adapt_row(pair):
            row_vec, adapter_id = pair
            low_rank = jnp.dot(row_vec[None, :], down_layer[adapter_id], preferred_element_type=jnp.float32)
            low_rank = low_rank.astype(jnp.bfloat16)
            return jnp.dot(low_rank, up_layer[adapter_id], preferred_element_type=jnp.float32)[0]

        delta_rows = lax.map(adapt_row, (rows_in, adapter_ids))
        mixed = jnp.where(live_rows[:, None], base_part + delta_rows, jnp.float32(0.0))
        results.append(mixed.astype(jnp.bfloat16))
    return jnp.stack(results)
```

```python
import functools

import jax
import jax.numpy as jnp
from jax import lax
from jax.experimental import pallas as pl
from jax.experimental.pallas import tpu as pltpu
from jax.sharding import PartitionSpec as P

CAP = 4
HALVES = 2
LANES = 128
F32 = jnp.float32
BF16 = jnp.bfloat16
VMEM = pl.BlockSpec(memory_space=pltpu.VMEM)
SMEM = pl.BlockSpec(memory_space=pltpu.SMEM)
HBM = pl.BlockSpec(memory_space=pl.ANY)
VMEM_LIMIT = 48 * 1024 * 1024


def iota(shape, axis):
    return lax.broadcasted_iota(jnp.int32, shape, axis)


def ranks(owner_row, stores):
    rows = owner_row.shape[1]
    me = lax.axis_index("store").astype(F32)
    down, across = iota((rows, rows), 0), iota((rows, rows), 1)
    owner_row = owner_row.astype(F32)
    spread = jnp.broadcast_to(owner_row, (rows, rows))
    owner_col = jnp.sum(jnp.where(down == across, spread, 0.0), axis=1, keepdims=True)
    same = owner_col == spread
    rank_row = jnp.sum(jnp.where(same & (down < across), 1.0, 0.0), axis=0, keepdims=True)
    rank_col = jnp.sum(jnp.where(same & (across < down), 1.0, 0.0), axis=1, keepdims=True)

    def hop(owner):
        return jnp.where(owner < me, owner - me + stores, owner - me)

    return hop(owner_row), rank_row, hop(owner_col), rank_col


def prepare_kernel(stores, owner_ref, slot_ref, x_ref, *out_refs):
    layers, rows, depth = x_ref.shape
    half = depth // HALVES
    block = layers * HALVES * CAP
    hop_row, rank_row, _, _ = ranks(owner_ref[...], stores)
    place = hop_row * block + rank_row
    places = jnp.concatenate([place + CAP * part for part in range(layers * HALVES)], axis=1)
    pick = iota((stores * block, layers * HALVES * rows), 0).astype(F32) == places
    stacked = jnp.concatenate(
        [
            x_ref[layer, :, part * half : (part + 1) * half]
            for layer in range(layers)
            for part in range(HALVES)
        ],
        axis=0,
    )
    sent = jnp.dot(pick.astype(BF16), stacked, preferred_element_type=F32).astype(BF16)
    first = iota((stores * block, rows), 0).astype(F32) == place
    slots = jnp.sum(
        jnp.where(first, jnp.broadcast_to(slot_ref[...].astype(F32), first.shape), 0.0),
        axis=1,
        keepdims=True,
    )
    slots = jnp.broadcast_to(slots, (stores * block, LANES)).astype(BF16)
    for k, out_ref in enumerate(out_refs):
        out_ref[:, :half] = sent[k * block : (k + 1) * block]
        out_ref[:, half:] = slots[k * block : (k + 1) * block]


def base_kernel(tensors, step, x_ref, w_hbm, *refs):
    out_refs, (w_ref, total_ref, sems) = refs[:tensors], refs[tensors:]
    layers, _, depth = x_ref.shape
    width = out_refs[0].shape[2]
    chunks = depth // step

    def fetch(layer, chunk):
        rows = pl.ds(chunk * step, step)
        return pltpu.make_async_copy(
            w_hbm.at[layer, rows], w_ref.at[layer, rows], sems.at[layer, chunk]
        )

    for layer in range(layers):
        for chunk in range(chunks):
            fetch(layer, chunk).start()
    for layer in range(layers):
        for chunk in range(chunks):
            fetch(layer, chunk).wait()
            part = jnp.dot(
                x_ref[layer, :, chunk * step : (chunk + 1) * step],
                w_ref[layer, chunk * step : (chunk + 1) * step, :],
                preferred_element_type=F32,
            )
            if chunk == 0:
                total_ref[layer] = part
            else:
                total_ref[layer] += part
    me = lax.axis_index("tensor")
    for j, out_ref in enumerate(out_refs):
        start = pl.multiple_of(lax.rem(me + j, tensors) * width, width)
        out_ref[...] = total_ref[:, :, pl.ds(start, width)]


def slot_of(block_ref, half, place):
    return block_ref[:, half:].astype(F32)[place, 0].astype(jnp.int32)


def down_kernel(stores, down_hbm, *refs):
    block_refs, (out_ref, w_ref, sems) = refs[:stores], refs[stores:]
    layers, _, rank, depth = down_hbm.shape
    half = depth // HALVES

    def fetch(layer, k, c, slot):
        return pltpu.make_async_copy(
            down_hbm.at[layer, slot],
            w_ref.at[layer, k, pl.ds(c * rank, rank)],
            sems.at[layer, k, c],
        )

    slots = [[slot_of(block_refs[k], half, c) for c in range(CAP)] for k in range(stores)]
    for layer in range(layers):
        for k in range(stores):
            for c in range(CAP):
                fetch(layer, k, c, slots[k][c]).start()
    block = layers * HALVES * CAP
    row, column = iota((block, CAP * rank), 0), iota((block, CAP * rank), 1)
    for layer in range(layers):
        for k in range(stores):
            for c in range(CAP):
                fetch(layer, k, c, slots[k][c]).wait()
            kept = jnp.zeros((block, CAP * rank), F32)
            for part in range(HALVES):
                product = lax.dot_general(
                    block_refs[k][:, :half],
                    w_ref[layer, k, :, part * half : (part + 1) * half],
                    (((1,), (1,)), ((), ())),
                    preferred_element_type=F32,
                )
                mine = row == (layer * HALVES + part) * CAP + column // rank
                kept = kept + jnp.where(mine, product, 0.0)
            at = layer * stores + k
            out_ref[at : at + 1, :] = jnp.sum(kept, axis=0, keepdims=True)


def up_kernel(stores, tensors, half, up_hbm, *refs):
    part_refs, refs = refs[:tensors], refs[tensors:]
    block_refs, refs = refs[:stores], refs[stores:]
    out_refs, (w_ref, sems) = refs[:stores], refs[stores:]
    layers, _, rank, width = up_hbm.shape

    def fetch(layer, k, c, slot):
        return pltpu.make_async_copy(
            up_hbm.at[layer, slot],
            w_ref.at[layer, k, pl.ds(c * rank, rank)],
            sems.at[layer, k, c],
        )

    slots = [[slot_of(block_refs[k], half, c) for c in range(CAP)] for k in range(stores)]
    for layer in range(layers):
        for k in range(stores):
            for c in range(CAP):
                fetch(layer, k, c, slots[k][c]).start()
    low = part_refs[0][...]
    for part_ref in part_refs[1:]:
        low = low + part_ref[...]
    row, column = iota((2 * CAP, CAP * rank), 0), iota((2 * CAP, CAP * rank), 1)
    own = row == column // rank
    for layer in range(layers):
        for k in range(stores):
            at = layer * stores + k
            spread = jnp.where(own, jnp.broadcast_to(low[at : at + 1, :], own.shape), 0.0)
            for c in range(CAP):
                fetch(layer, k, c, slots[k][c]).wait()
            terms = jnp.dot(spread.astype(BF16), w_ref[layer, k], preferred_element_type=F32)
            out_refs[k][layer * CAP : (layer + 1) * CAP, :] = terms[:CAP]


def final_kernel(stores, tensors, count_ref, owner_ref, *refs):
    base_refs, term_refs, out_ref = refs[:tensors], refs[tensors : tensors + stores], refs[-1]
    layers, rows, _ = out_ref.shape
    _, _, hop_col, rank_col = ranks(owner_ref[...], stores)
    terms = jnp.concatenate([term_ref[...] for term_ref in term_refs], axis=0)
    live = iota((rows, 1), 0) < count_ref[0]
    for layer in range(layers):
        total = base_refs[0][layer]
        for base_ref in base_refs[1:]:
            total = total + base_ref[layer]
        place = hop_col * (layers * CAP) + layer * CAP + rank_col
        pick = iota((rows, stores * layers * CAP), 1).astype(F32) == place
        delta = jnp.dot(
            pick.astype(F32), terms, preferred_element_type=F32, precision=lax.Precision.HIGHEST
        )
        out_ref[layer] = jnp.where(live, total + delta, 0.0).astype(BF16)


def params():
    return pltpu.CompilerParams(vmem_limit_bytes=VMEM_LIMIT)


def local(stores, tensors, x, w, down, up, owner, slot, count):
    layers, rows, depth = x.shape
    adapters, rank, width = up.shape[1:]
    half = depth // HALVES
    block = layers * HALVES * CAP
    owner_row = owner.reshape(1, rows)
    slot_row = slot.reshape(1, rows)
    down = jnp.swapaxes(down, 2, 3)

    def shift(value, axis, size, by):
        if by % size == 0:
            return value
        return lax.ppermute(value, axis, [(i, (i + by) % size) for i in range(size)])

    payloads = pl.pallas_call(
        functools.partial(prepare_kernel, stores),
        out_shape=[jax.ShapeDtypeStruct((block, half + LANES), BF16)] * stores,
        in_specs=[VMEM] * 3,
        out_specs=[VMEM] * stores,
        compiler_params=params(),
        cost_estimate=pl.CostEstimate(
            flops=0, bytes_accessed=4 * layers * rows * depth, transcendentals=0
        ),
        name="prepare",
    )(owner_row, slot_row, x)
    blocks = [shift(payloads[k], "store", stores, k) for k in range(stores)]

    step = min(256, depth)
    base = pl.pallas_call(
        functools.partial(base_kernel, tensors, step),
        out_shape=[jax.ShapeDtypeStruct((layers, rows, width), F32)] * tensors,
        in_specs=[VMEM, HBM],
        out_specs=[VMEM] * tensors,
        scratch_shapes=[
            pltpu.VMEM(w.shape, BF16),
            pltpu.VMEM((layers, rows, w.shape[2]), F32),
            pltpu.SemaphoreType.DMA((layers, depth // step)),
        ],
        compiler_params=params(),
        cost_estimate=pl.CostEstimate(
            flops=2 * rows * w.size, bytes_accessed=2 * w.size, transcendentals=0
        ),
        name="base",
    )(x, w)
    sums = [shift(base[j], "tensor", tensors, j) for j in range(tensors)]

    low = pl.pallas_call(
        functools.partial(down_kernel, stores),
        out_shape=jax.ShapeDtypeStruct((layers * stores, CAP * rank), F32),
        in_specs=[HBM] + [VMEM] * stores,
        out_specs=VMEM,
        scratch_shapes=[
            pltpu.VMEM((layers, stores, CAP * rank, depth), BF16),
            pltpu.SemaphoreType.DMA((layers, stores, CAP)),
        ],
        compiler_params=params(),
        cost_estimate=pl.CostEstimate(
            flops=0, bytes_accessed=2 * layers * stores * CAP * rank * depth, transcendentals=0
        ),
        name="down",
    )(down, *blocks)
    lows = [shift(low, "tensor", tensors, j) for j in range(tensors)]

    terms = pl.pallas_call(
        functools.partial(up_kernel, stores, tensors, half),
        out_shape=[jax.ShapeDtypeStruct((layers * CAP, width), F32)] * stores,
        in_specs=[HBM] + [VMEM] * (tensors + stores),
        out_specs=[VMEM] * stores,
        scratch_shapes=[
            pltpu.VMEM((layers, stores, CAP * rank, width), BF16),
            pltpu.SemaphoreType.DMA((layers, stores, CAP)),
        ],
        compiler_params=params(),
        cost_estimate=pl.CostEstimate(
            flops=0, bytes_accessed=2 * layers * stores * CAP * rank * width, transcendentals=0
        ),
        name="up",
    )(up, *lows, *blocks)
    returned = [shift(terms[k], "store", stores, -k) for k in range(stores)]

    return pl.pallas_call(
        functools.partial(final_kernel, stores, tensors),
        out_shape=jax.ShapeDtypeStruct((layers, rows, width), BF16),
        in_specs=[SMEM] + [VMEM] * (1 + tensors + stores),
        out_specs=VMEM,
        compiler_params=params(),
        cost_estimate=pl.CostEstimate(
            flops=0, bytes_accessed=8 * layers * rows * width * tensors, transcendentals=0
        ),
        name="final",
    )(count, owner_row, *sums, *returned)


def solution(mesh):
    return jax.shard_map(
        functools.partial(local, mesh.shape["store"], mesh.shape["tensor"]),
        mesh=mesh,
        in_specs=(
            P(None, ("groups", "store"), "tensor"),
            P(None, "tensor", None),
            P(None, "store", "tensor", None),
            P(None, "store", None, "tensor"),
            P(("groups", "store"), None),
            P(("groups", "store")),
            P(("groups", "store")),
        ),
        out_specs=P(None, ("groups", "store"), "tensor"),
        check_vma=False,
    )
```

```python
import functools

import jax
import jax.numpy as jnp
from jax import lax
from jax.experimental import pallas as pl
from jax.experimental.pallas import tpu as pltpu
from jax.sharding import PartitionSpec as P

CAP = 4
HALVES = 2
LANES = 128
F32 = jnp.float32
BF16 = jnp.bfloat16
VMEM = pl.BlockSpec(memory_space=pltpu.VMEM)
SMEM = pl.BlockSpec(memory_space=pltpu.SMEM)
HBM = pl.BlockSpec(memory_space=pl.ANY)
VMEM_LIMIT = 8 * 1024 * 1024


def iota(shape, axis):
    return lax.broadcasted_iota(jnp.int32, shape, axis)


def ranks(owner_row):
    rows = owner_row.shape[1]
    down, across = iota((rows, rows), 0), iota((rows, rows), 1)
    owner_row = (owner_row ^ lax.axis_index("store")).astype(F32)
    spread = jnp.broadcast_to(owner_row, (rows, rows))
    owner_col = jnp.sum(jnp.where(down == across, spread, 0.0), axis=1, keepdims=True)
    same = owner_col == spread
    rank_row = jnp.sum(jnp.where(same & (down < across), 1.0, 0.0), axis=0, keepdims=True)
    rank_col = jnp.sum(jnp.where(same & (across < down), 1.0, 0.0), axis=1, keepdims=True)
    return owner_row, rank_row, owner_col, rank_col


def prepare_kernel(stores, owner_hbm, slot_hbm, x_hbm, *refs):
    out_refs, (owner_ref, slot_ref, x_ref, sems) = refs[:stores], refs[stores:]
    pairs = ((owner_hbm, owner_ref), (slot_hbm, slot_ref), (x_hbm, x_ref))
    copies = [
        pltpu.make_async_copy(source, target, sems.at[i]) for i, (source, target) in enumerate(pairs)
    ]
    for copy in copies:
        copy.start()
    for copy in copies:
        copy.wait()
    layers, rows, depth = x_ref.shape
    half = depth // HALVES
    block = layers * HALVES * CAP
    hop_row, rank_row, _, _ = ranks(owner_ref[...])
    place = hop_row * block + rank_row
    places = jnp.concatenate([place + CAP * part for part in range(layers * HALVES)], axis=1)
    pick = iota((stores * block, layers * HALVES * rows), 0).astype(F32) == places
    stacked = jnp.concatenate(
        [
            x_ref[layer, :, part * half : (part + 1) * half]
            for layer in range(layers)
            for part in range(HALVES)
        ],
        axis=0,
    )
    sent = jnp.dot(pick.astype(BF16), stacked, preferred_element_type=F32).astype(BF16)
    first = iota((stores * block, rows), 0).astype(F32) == place
    slots = jnp.sum(
        jnp.where(first, jnp.broadcast_to(slot_ref[...].astype(F32), first.shape), 0.0),
        axis=1,
        keepdims=True,
    )
    slots = jnp.broadcast_to(slots, (stores * block, LANES)).astype(BF16)
    for k, out_ref in enumerate(out_refs):
        out_ref[:, :half] = sent[k * block : (k + 1) * block]
        out_ref[:, half:] = slots[k * block : (k + 1) * block]


def chunk_order(tensors):
    if tensors == 1:
        return [0]
    rest = [2 * mask for mask in chunk_order(tensors // 2)]
    return rest + [mask + 1 for mask in rest]


def base_kernel(tensors, _, x_ref, w_ref, keep_ref, send_ref):
    layers = x_ref.shape[0]
    width = keep_ref.shape[3]
    me = lax.axis_index("tensor")
    for i, mask in enumerate(chunk_order(tensors)):
        out_ref = keep_ref if i < tensors // 2 else send_ref
        columns = pl.ds(pl.multiple_of((me ^ mask) * width, width), width)
        for layer in range(layers):
            out_ref[i % (tensors // 2), layer] = jnp.dot(
                x_ref[layer], w_ref[layer, :, columns], preferred_element_type=F32
            )


def down_kernel(stores, down_ref, *refs):
    block_refs, (low_ref, slot_ref) = refs[:stores], refs[stores:]
    layers, _, rank, depth = down_ref.shape
    half = depth // HALVES
    block = layers * HALVES * CAP
    row, column = iota((CAP * rank, block), 0), iota((CAP * rank, block), 1)
    columns = []
    for k in range(stores):
        tail = block_refs[k][:, half:].astype(F32)
        slots = [tail[c, 0].astype(jnp.int32) for c in range(CAP)]
        for c in range(CAP):
            slot_ref[k * CAP + c] = slots[c]
        total = jnp.zeros((rank, block), F32)
        for layer in range(layers):
            for part in range(HALVES):
                span = slice(part * half, (part + 1) * half)
                chosen = jnp.concatenate([down_ref[layer, slot, :, span] for slot in slots], axis=0)
                product = lax.dot_general(
                    chosen,
                    block_refs[k][:, :half],
                    (((1,), (1,)), ((), ())),
                    preferred_element_type=F32,
                )
                mine = column == (layer * HALVES + part) * CAP + row // rank
                product = jnp.where(mine, product, 0.0)
                for c in range(CAP):
                    total = total + product[c * rank : (c + 1) * rank]
        columns.append(total)
    turned = jnp.concatenate(columns, axis=1).T
    for k in range(stores):
        for layer in range(layers):
            at = k * block + layer * HALVES * CAP
            low_ref[(k * layers + layer) * CAP : (k * layers + layer + 1) * CAP] = (
                turned[at : at + CAP] + turned[at + CAP : at + 2 * CAP]
            )


def up_kernel(stores, tensors, slot_ref, up_ref, keep_ref, got_ref, *refs):
    low_refs, refs = refs[:tensors], refs[tensors:]
    out_refs, (own_ref, send_ref) = refs[:stores], refs[stores:]
    layers, _, rank, width = up_ref.shape
    low = low_refs[0][...]
    for low_ref in low_refs[1:]:
        low = low + low_ref[...]
    row, column = iota((CAP, CAP * rank), 0), iota((CAP, CAP * rank), 1)
    for k in range(stores):
        for layer in range(layers):
            at = (k * layers + layer) * CAP
            spread = jnp.concatenate([low[at : at + CAP]] * CAP, axis=1)
            spread = jnp.where(row == column // rank, spread, 0.0).astype(BF16)
            chosen = jnp.concatenate(
                [up_ref[layer, slot_ref[k * CAP + c]] for c in range(CAP)], axis=0
            )
            out_refs[k][layer * CAP : (layer + 1) * CAP, :] = jnp.dot(
                spread, chosen, preferred_element_type=F32
            )
    own_ref[...] = keep_ref[0] + got_ref[0]
    send_ref[...] = keep_ref[1] + got_ref[1]


def final_kernel(stores, count_ref, owner_ref, own_ref, got_ref, *refs):
    term_refs, out_ref = refs[:stores], refs[-1]
    layers, rows, _ = out_ref.shape
    _, _, hop_col, rank_col = ranks(owner_ref[...])
    terms = jnp.concatenate([term_ref[...] for term_ref in term_refs], axis=0)
    live = iota((rows, 1), 0) < count_ref[0]
    for layer in range(layers):
        total = own_ref[layer] + got_ref[layer]
        place = hop_col * (layers * CAP) + layer * CAP + rank_col
        pick = iota((rows, stores * layers * CAP), 1).astype(F32) == place
        delta = jnp.dot(
            pick.astype(F32), terms, preferred_element_type=F32, precision=lax.Precision.HIGHEST
        )
        out_ref[layer] = jnp.where(live, total + delta, 0.0).astype(BF16)


def params():
    return pltpu.CompilerParams(vmem_limit_bytes=VMEM_LIMIT)


def cost(microseconds):
    return pl.CostEstimate(
        flops=int(microseconds * 1.1535e9), bytes_accessed=0, transcendentals=0
    )


def local(stores, tensors, x, w, down, up, owner, slot, count):
    layers, rows, depth = x.shape
    adapters, rank, width = up.shape[1:]
    half = depth // HALVES
    block = layers * HALVES * CAP
    owner_row = owner.reshape(1, rows)
    slot_row = slot.reshape(1, rows)
    down = jnp.swapaxes(down, 2, 3)

    def swap(value, axis, size, by):
        if by == 0:
            return value
        return lax.ppermute(value, axis, [(i, i ^ by) for i in range(size)])

    payloads = pl.pallas_call(
        functools.partial(prepare_kernel, stores),
        out_shape=[jax.ShapeDtypeStruct((block, half + LANES), BF16)] * stores,
        in_specs=[HBM] * 3,
        out_specs=[VMEM] * stores,
        scratch_shapes=[
            pltpu.VMEM((1, rows), jnp.int32),
            pltpu.VMEM((1, rows), jnp.int32),
            pltpu.VMEM(x.shape, BF16),
            pltpu.SemaphoreType.DMA((3,)),
        ],
        compiler_params=params(),
        cost_estimate=cost(6),
        name="prepare",
    )(owner_row, slot_row, x)
    blocks = [swap(payloads[k], "store", stores, k) for k in range(stores)]

    keep, send = pl.pallas_call(
        functools.partial(base_kernel, tensors),
        out_shape=[jax.ShapeDtypeStruct((tensors // 2, layers, rows, width), F32)] * 2,
        in_specs=[HBM] + [VMEM] * 2,
        out_specs=[VMEM] * 2,
        compiler_params=params(),
        cost_estimate=cost(6),
        name="base",
    )(payloads[0], x, w)
    got = swap(send, "tensor", tensors, 1)
    bit = 2
    while keep.shape[0] > 2:
        total, middle = keep + got, keep.shape[0] // 2
        keep, got = total[:middle], swap(total[middle:], "tensor", tensors, bit)
        bit *= 2

    low, slots = pl.pallas_call(
        functools.partial(down_kernel, stores),
        out_shape=[
            jax.ShapeDtypeStruct((stores * layers * CAP, rank), F32),
            jax.ShapeDtypeStruct((stores * CAP,), jnp.int32),
        ],
        in_specs=[VMEM] * (1 + stores),
        out_specs=[VMEM, SMEM],
        compiler_params=params(),
        cost_estimate=cost(4),
        name="down",
    )(down, *blocks)
    lows = [swap(low, "tensor", tensors, j) for j in range(tensors)]

    *terms, own, send = pl.pallas_call(
        functools.partial(up_kernel, stores, tensors),
        out_shape=[jax.ShapeDtypeStruct((layers * CAP, width), F32)] * stores
        + [jax.ShapeDtypeStruct((layers, rows, width), F32)] * 2,
        in_specs=[SMEM] + [VMEM] * (3 + tensors),
        out_specs=[VMEM] * (stores + 2),
        compiler_params=params(),
        cost_estimate=cost(1),
        name="up",
    )(slots, up, keep, got, *lows)
    returned = [swap(terms[k], "store", stores, k) for k in range(stores)]
    got = swap(send, "tensor", tensors, bit)

    return pl.pallas_call(
        functools.partial(final_kernel, stores),
        out_shape=jax.ShapeDtypeStruct((layers, rows, width), BF16),
        in_specs=[SMEM] + [VMEM] * (3 + stores),
        out_specs=VMEM,
        compiler_params=params(),
        cost_estimate=cost(1),
        name="final",
    )(count, owner_row, own, got, *returned)


def solution(mesh):
    return jax.shard_map(
        functools.partial(local, mesh.shape["store"], mesh.shape["tensor"]),
        mesh=mesh,
        in_specs=(
            P(None, ("groups", "store"), "tensor"),
            P(None, "tensor", None),
            P(None, "store", "tensor", None),
            P(None, "store", None, "tensor"),
            P(("groups", "store"), None),
            P(("groups", "store")),
            P(("groups", "store")),
        ),
        out_specs=P(None, ("groups", "store"), "tensor"),
        check_vma=False,
    )
```

```python
import functools

import jax
import jax.numpy as jnp
from jax import lax
from jax.experimental import pallas as pl
from jax.experimental.pallas import tpu as pltpu
from jax.sharding import PartitionSpec as P

CAP = 4
HALVES = 2
LANES = 128
PIECES = 3
F32 = jnp.float32
BF16 = jnp.bfloat16
VMEM = pl.BlockSpec(memory_space=pltpu.VMEM)
SMEM = pl.BlockSpec(memory_space=pltpu.SMEM)
HBM = pl.BlockSpec(memory_space=pltpu.HBM)
ANY = pl.BlockSpec(memory_space=pl.ANY)
SMALL = 8 * 1024 * 1024
LARGE = 48 * 1024 * 1024


def iota(shape, axis):
    return lax.broadcasted_iota(jnp.int32, shape, axis)


def ranks(owner_row):
    rows = owner_row.shape[1]
    down, across = iota((rows, rows), 0), iota((rows, rows), 1)
    owner_row = (owner_row ^ lax.axis_index("store")).astype(F32)
    spread = jnp.broadcast_to(owner_row, (rows, rows))
    owner_col = jnp.sum(jnp.where(down == across, spread, 0.0), axis=1, keepdims=True)
    same = owner_col == spread
    rank_row = jnp.sum(jnp.where(same & (down < across), 1.0, 0.0), axis=0, keepdims=True)
    rank_col = jnp.sum(jnp.where(same & (across < down), 1.0, 0.0), axis=1, keepdims=True)
    return owner_row, rank_row, owner_col, rank_col


def prepare_kernel(stores, owner_hbm, slot_hbm, x_hbm, *refs):
    out_refs, (pick_ref, owner_ref, slot_ref, x_ref, sems) = refs[:stores], refs[stores:]
    pairs = ((owner_hbm, owner_ref), (slot_hbm, slot_ref), (x_hbm, x_ref))
    copies = [
        pltpu.make_async_copy(source, target, sems.at[i]) for i, (source, target) in enumerate(pairs)
    ]
    for copy in copies:
        copy.start()
    for copy in copies:
        copy.wait()
    layers, rows, depth = x_ref.shape
    half = depth // HALVES
    block = layers * HALVES * CAP
    hop_row, rank_row, hop_col, rank_col = ranks(owner_ref[...])
    place = hop_row * block + rank_row
    places = jnp.concatenate([place + CAP * part for part in range(layers * HALVES)], axis=1)
    pick = iota((stores * block, layers * HALVES * rows), 0).astype(F32) == places
    stacked = jnp.concatenate(
        [
            x_ref[layer, :, part * half : (part + 1) * half]
            for layer in range(layers)
            for part in range(HALVES)
        ],
        axis=0,
    )
    sent = jnp.dot(pick.astype(BF16), stacked, preferred_element_type=F32).astype(BF16)
    first = iota((stores * block, rows), 0).astype(F32) == place
    slots = jnp.sum(
        jnp.where(first, jnp.broadcast_to(slot_ref[...].astype(F32), first.shape), 0.0),
        axis=1,
        keepdims=True,
    )
    slots = jnp.broadcast_to(slots, (stores * block, LANES)).astype(BF16)
    for k, out_ref in enumerate(out_refs):
        out_ref[:, :half] = sent[k * block : (k + 1) * block]
        out_ref[:, half:] = slots[k * block : (k + 1) * block]
    spots = lax.rem(iota((rows, pick_ref.shape[1]), 1), stores * layers * CAP).astype(F32)
    place = hop_col * (layers * CAP) + rank_col
    for layer in range(layers):
        pick_ref[layer * rows : (layer + 1) * rows] = (spots == place + layer * CAP).astype(BF16)


def chunk_order(tensors):
    if tensors == 1:
        return [0]
    rest = [2 * mask for mask in chunk_order(tensors // 2)]
    return rest + [mask + 1 for mask in rest]


def base_kernel(tensors, _, x_ref, w_ref, keep_ref, send_ref):
    layers = x_ref.shape[0]
    width = keep_ref.shape[3]
    me = lax.axis_index("tensor")
    for i, mask in enumerate(chunk_order(tensors)):
        out_ref = keep_ref if i < tensors // 2 else send_ref
        columns = pl.ds(pl.multiple_of((me ^ mask) * width, width), width)
        for layer in range(layers):
            out_ref[i % (tensors // 2), layer] = jnp.dot(
                x_ref[layer], w_ref[layer, :, columns], preferred_element_type=F32
            )


def down_kernel(stores, down_hbm, *refs):
    block_refs, (low_ref, slot_ref, w_ref, sems) = refs[:stores], refs[stores:]
    layers, _, rank, depth = down_hbm.shape
    half = depth // HALVES
    block = layers * HALVES * CAP

    def fetch(layer, k, c, slot):
        return pltpu.make_async_copy(
            down_hbm.at[layer, slot],
            w_ref.at[layer, k, pl.ds(c * rank, rank)],
            sems.at[layer, k, c],
        )

    slots = []
    for k in range(stores):
        tail = block_refs[k][:, half:].astype(F32)
        slots.append([tail[c, 0].astype(jnp.int32) for c in range(CAP)])
        for c in range(CAP):
            slot_ref[k * CAP + c] = slots[k][c]
            for layer in range(layers):
                fetch(layer, k, c, slots[k][c]).start()
    row, column = iota((CAP * rank, block), 0), iota((CAP * rank, block), 1)
    columns = []
    for k in range(stores):
        for c in range(CAP):
            for layer in range(layers):
                fetch(layer, k, c, slots[k][c]).wait()
        total = jnp.zeros((rank, block), F32)
        for layer in range(layers):
            for part in range(HALVES):
                product = lax.dot_general(
                    w_ref[layer, k, :, part * half : (part + 1) * half],
                    block_refs[k][:, :half],
                    (((1,), (1,)), ((), ())),
                    preferred_element_type=F32,
                )
                mine = column == (layer * HALVES + part) * CAP + row // rank
                product = jnp.where(mine, product, 0.0)
                for c in range(CAP):
                    total = total + product[c * rank : (c + 1) * rank]
        columns.append(total)
    turned = jnp.concatenate(columns, axis=1).T
    for k in range(stores):
        for layer in range(layers):
            at = k * block + layer * HALVES * CAP
            low_ref[(k * layers + layer) * CAP : (k * layers + layer + 1) * CAP] = (
                turned[at : at + CAP] + turned[at + CAP : at + 2 * CAP]
            )


def pair_kernel(_, keep_ref, got_ref, own_ref, send_ref):
    own_ref[...] = keep_ref[0] + got_ref[0]
    send_ref[...] = keep_ref[1] + got_ref[1]


def up_kernel(stores, tensors, _, slot_ref, up_ref, *refs):
    low_refs, out_refs = refs[:tensors], refs[tensors:]
    layers, _, rank, width = up_ref.shape
    low = low_refs[0][...]
    for low_ref in low_refs[1:]:
        low = low + low_ref[...]
    row, column = iota((CAP, CAP * rank), 0), iota((CAP, CAP * rank), 1)
    for k in range(stores):
        for layer in range(layers):
            at = (k * layers + layer) * CAP
            spread = jnp.concatenate([low[at : at + CAP]] * CAP, axis=1)
            spread = jnp.where(row == column // rank, spread, 0.0).astype(BF16)
            chosen = jnp.concatenate(
                [up_ref[layer, slot_ref[k * CAP + c]] for c in range(CAP)], axis=0
            )
            out_refs[k][layer * CAP : (layer + 1) * CAP, :] = jnp.dot(
                spread, chosen, preferred_element_type=F32
            )


def final_kernel(count_ref, pick_ref, own_ref, got_ref, *refs):
    term_refs, out_ref = refs[:-1], refs[-1]
    layers, rows, _ = out_ref.shape
    terms = jnp.concatenate([term_ref[...] for term_ref in term_refs], axis=0)
    pieces = []
    for _ in range(PIECES):
        pieces.append(terms.astype(BF16))
        terms = terms - pieces[-1].astype(F32)
    delta = jnp.dot(
        pick_ref[...], jnp.concatenate(pieces, axis=0), preferred_element_type=F32
    )
    live = iota((rows, 1), 0) < count_ref[0]
    for layer in range(layers):
        total = own_ref[layer] + got_ref[layer] + delta[layer * rows : (layer + 1) * rows]
        out_ref[layer] = jnp.where(live, total, 0.0).astype(BF16)


def params(limit=SMALL):
    return pltpu.CompilerParams(vmem_limit_bytes=limit)


def cost(microseconds):
    return pl.CostEstimate(
        flops=int(microseconds * 1.1535e9), bytes_accessed=0, transcendentals=0
    )


def local(stores, tensors, x, w, down, up, owner, slot, count):
    layers, rows, depth = x.shape
    adapters, rank, width = up.shape[1:]
    half = depth // HALVES
    block = layers * HALVES * CAP
    owner_row = owner.reshape(1, rows)
    slot_row = slot.reshape(1, rows)
    down = jnp.swapaxes(down, 2, 3)

    def swap(value, axis, size, by):
        if by == 0:
            return value
        return lax.ppermute(value, axis, [(i, i ^ by) for i in range(size)])

    *payloads, pick = pl.pallas_call(
        functools.partial(prepare_kernel, stores),
        out_shape=[jax.ShapeDtypeStruct((block, half + LANES), BF16)] * stores
        + [
            jax.ShapeDtypeStruct((layers * rows, PIECES * stores * layers * CAP), BF16),
        ],
        in_specs=[ANY] * 3,
        out_specs=[VMEM] * (stores + 1),
        scratch_shapes=[
            pltpu.VMEM((1, rows), jnp.int32),
            pltpu.VMEM((1, rows), jnp.int32),
            pltpu.VMEM(x.shape, BF16),
            pltpu.SemaphoreType.DMA((3,)),
        ],
        compiler_params=params(),
        cost_estimate=cost(6),
        name="prepare",
    )(*(pltpu.with_memory_space_constraint(v, pltpu.HBM) for v in (owner_row, slot_row, x)))
    blocks = [swap(payloads[k], "store", stores, k) for k in range(stores)]

    keep, send = pl.pallas_call(
        functools.partial(base_kernel, tensors),
        out_shape=[jax.ShapeDtypeStruct((tensors // 2, layers, rows, width), F32)] * 2,
        in_specs=[ANY] + [VMEM] * 2,
        out_specs=[VMEM] * 2,
        compiler_params=params(),
        cost_estimate=cost(6),
        name="base",
    )(payloads[0], x, w)
    got = swap(send, "tensor", tensors, 1)
    bit = 2
    while keep.shape[0] > 2:
        total, middle = keep + got, keep.shape[0] // 2
        keep, got = total[:middle], swap(total[middle:], "tensor", tensors, bit)
        bit *= 2

    low, slots = pl.pallas_call(
        functools.partial(down_kernel, stores),
        out_shape=[
            jax.ShapeDtypeStruct((stores * layers * CAP, rank), F32),
            jax.ShapeDtypeStruct((stores * CAP,), jnp.int32),
        ],
        in_specs=[HBM] + [VMEM] * stores,
        out_specs=[VMEM, SMEM],
        scratch_shapes=[
            pltpu.VMEM((layers, stores, CAP * rank, depth), BF16),
            pltpu.SemaphoreType.DMA((layers, stores, CAP)),
        ],
        compiler_params=params(LARGE),
        cost_estimate=cost(4),
        name="down",
    )(down, *blocks)
    lows = [swap(low, "tensor", tensors, j) for j in range(tensors)]
    own, send = pl.pallas_call(
        pair_kernel,
        out_shape=[jax.ShapeDtypeStruct((layers, rows, width), F32)] * 2,
        in_specs=[ANY] + [VMEM] * 2,
        out_specs=[VMEM] * 2,
        compiler_params=params(),
        cost_estimate=cost(0.3),
        name="pair",
    )(low, keep, got)
    got = swap(send, "tensor", tensors, bit)

    terms = pl.pallas_call(
        functools.partial(up_kernel, stores, tensors),
        out_shape=[jax.ShapeDtypeStruct((layers * CAP, width), F32)] * stores,
        in_specs=[ANY, SMEM] + [VMEM] * (1 + tensors),
        out_specs=[VMEM] * stores,
        compiler_params=params(),
        cost_estimate=cost(1),
        name="up",
    )(own, slots, up, *lows)
    returned = [swap(terms[k], "store", stores, k) for k in range(stores)]

    return pl.pallas_call(
        final_kernel,
        out_shape=jax.ShapeDtypeStruct((layers, rows, width), BF16),
        in_specs=[SMEM] + [VMEM] * (3 + stores),
        out_specs=VMEM,
        compiler_params=params(),
        cost_estimate=cost(1),
        name="final",
    )(count, pick, own, got, *returned)


def solution(mesh):
    return jax.shard_map(
        functools.partial(local, mesh.shape["store"], mesh.shape["tensor"]),
        mesh=mesh,
        in_specs=(
            P(None, ("groups", "store"), "tensor"),
            P(None, "tensor", None),
            P(None, "store", "tensor", None),
            P(None, "store", None, "tensor"),
            P(("groups", "store"), None),
            P(("groups", "store")),
            P(("groups", "store")),
        ),
        out_specs=P(None, ("groups", "store"), "tensor"),
        check_vma=False,
    )
```

```python
import functools

import jax
import jax.numpy as jnp
from jax import lax
from jax.experimental import pallas as pl
from jax.experimental.pallas import tpu as pltpu
from jax.sharding import PartitionSpec as P

CAP = 4
HALVES = 2
LANES = 128
PIECES = 3
F32 = jnp.float32
BF16 = jnp.bfloat16
VMEM = pl.BlockSpec(memory_space=pltpu.VMEM)
SMEM = pl.BlockSpec(memory_space=pltpu.SMEM)
HBM = pl.BlockSpec(memory_space=pltpu.HBM)
ANY = pl.BlockSpec(memory_space=pl.ANY)
SMALL = 8 * 1024 * 1024
LARGE = 24 * 1024 * 1024


def iota(shape, axis):
    return lax.broadcasted_iota(jnp.int32, shape, axis)


def ranks(owner_row):
    rows = owner_row.shape[1]
    down, across = iota((rows, rows), 0), iota((rows, rows), 1)
    owner_row = (owner_row ^ lax.axis_index("store")).astype(F32)
    spread = jnp.broadcast_to(owner_row, (rows, rows))
    owner_col = jnp.sum(jnp.where(down == across, spread, 0.0), axis=1, keepdims=True)
    same = owner_col == spread
    rank_row = jnp.sum(jnp.where(same & (down < across), 1.0, 0.0), axis=0, keepdims=True)
    rank_col = jnp.sum(jnp.where(same & (across < down), 1.0, 0.0), axis=1, keepdims=True)
    return owner_row, rank_row, owner_col, rank_col


def prepare_kernel(stores, owner_hbm, slot_hbm, x_hbm, *refs):
    out_refs, (pick_ref, owner_ref, slot_ref, x_ref, sems) = refs[:stores], refs[stores:]
    pairs = ((owner_hbm, owner_ref), (slot_hbm, slot_ref), (x_hbm, x_ref))
    copies = [
        pltpu.make_async_copy(source, target, sems.at[i]) for i, (source, target) in enumerate(pairs)
    ]
    for copy in copies:
        copy.start()
    for copy in copies:
        copy.wait()
    layers, rows, depth = x_ref.shape
    half = depth // HALVES
    block = layers * HALVES * CAP
    hop_row, rank_row, hop_col, rank_col = ranks(owner_ref[...])
    place = hop_row * block + rank_row
    places = jnp.concatenate([place + CAP * part for part in range(layers * HALVES)], axis=1)
    pick = iota((stores * block, layers * HALVES * rows), 0).astype(F32) == places
    stacked = jnp.concatenate(
        [
            x_ref[layer, :, part * half : (part + 1) * half]
            for layer in range(layers)
            for part in range(HALVES)
        ],
        axis=0,
    )
    sent = jnp.dot(pick.astype(BF16), stacked, preferred_element_type=F32).astype(BF16)
    first = iota((stores * block, rows), 0).astype(F32) == place
    slots = jnp.sum(
        jnp.where(first, jnp.broadcast_to(slot_ref[...].astype(F32), first.shape), 0.0),
        axis=1,
        keepdims=True,
    )
    slots = jnp.broadcast_to(slots, (stores * block, LANES)).astype(BF16)
    for k, out_ref in enumerate(out_refs):
        out_ref[:, :half] = sent[k * block : (k + 1) * block]
        out_ref[:, half:] = slots[k * block : (k + 1) * block]
    spots = lax.rem(iota((rows, pick_ref.shape[1]), 1), stores * layers * CAP).astype(F32)
    place = hop_col * (layers * CAP) + rank_col
    for layer in range(layers):
        pick_ref[layer * rows : (layer + 1) * rows] = (spots == place + layer * CAP).astype(BF16)


def chunk_order(tensors):
    if tensors == 1:
        return [0]
    rest = [2 * mask for mask in chunk_order(tensors // 2)]
    return rest + [mask + 1 for mask in rest]


def slots_of(block_ref, half):
    tail = block_ref[:, half:].astype(F32)
    return [tail[c, 0].astype(jnp.int32) for c in range(CAP)]


def fetches(store_hbm, slots, chosen_ref, sems):
    layers, _, rank, _ = store_hbm.shape
    return [
        pltpu.make_async_copy(
            store_hbm.at[layer, slot],
            chosen_ref.at[layer, pl.ds(c * rank, rank)],
            sems.at[layer, c],
        )
        for layer in range(layers)
        for c, slot in enumerate(slots)
    ]


def base_kernel(tensors, early, down_hbm, x_ref, w_ref, *refs):
    block_refs, (keep_ref, send_ref, chosen_ref, sems) = refs[:early], refs[early:]
    layers, _, depth = x_ref.shape
    width = keep_ref.shape[3]
    copies = []
    for i, block_ref in enumerate(block_refs):
        slots = slots_of(block_ref, depth // HALVES)
        copies += fetches(down_hbm, slots, chosen_ref.at[i], sems.at[i])
    for copy in copies:
        copy.start()
    me = lax.axis_index("tensor")
    for i, mask in enumerate(chunk_order(tensors)):
        out_ref = keep_ref if i < tensors // 2 else send_ref
        columns = pl.ds(pl.multiple_of((me ^ mask) * width, width), width)
        for layer in range(layers):
            out_ref[i % (tensors // 2), layer] = jnp.dot(
                x_ref[layer], w_ref[layer, :, columns], preferred_element_type=F32
            )
    for copy in copies:
        copy.wait()


def down_kernel(order, early, down_hbm, early_ref, *refs):
    stores = len(order)
    block_refs, (low_ref, slot_ref, late_ref, sems) = refs[:stores], refs[stores:]
    layers, _, rank, depth = down_hbm.shape
    half = depth // HALVES
    block = layers * HALVES * CAP
    slots = [slots_of(block_ref, half) for block_ref in block_refs]
    copies = [
        fetches(down_hbm, slots[i], late_ref.at[i - early], sems.at[i - early])
        for i in range(early, stores)
    ]
    for group in copies:
        for copy in group:
            copy.start()
    for i, k in enumerate(order):
        for c in range(CAP):
            slot_ref[k * CAP + c] = slots[i][c]
    row, column = iota((CAP * rank, block), 0), iota((CAP * rank, block), 1)
    columns = {}
    for i, k in enumerate(order):
        chosen_ref = early_ref.at[i] if i < early else late_ref.at[i - early]
        if i >= early:
            for copy in copies[i - early]:
                copy.wait()
        total = jnp.zeros((rank, block), F32)
        for layer in range(layers):
            for part in range(HALVES):
                product = lax.dot_general(
                    chosen_ref[layer, :, part * half : (part + 1) * half],
                    block_refs[i][:, :half],
                    (((1,), (1,)), ((), ())),
                    preferred_element_type=F32,
                )
                mine = column == (layer * HALVES + part) * CAP + row // rank
                product = jnp.where(mine, product, 0.0)
                for c in range(CAP):
                    total = total + product[c * rank : (c + 1) * rank]
        columns[k] = total
    turned = jnp.concatenate([columns[k] for k in range(stores)], axis=1).T
    for k in range(stores):
        for layer in range(layers):
            at = k * block + layer * HALVES * CAP
            low_ref[(k * layers + layer) * CAP : (k * layers + layer + 1) * CAP] = (
                turned[at : at + CAP] + turned[at + CAP : at + 2 * CAP]
            )


def pair_kernel(_, keep_ref, got_ref, own_ref, send_ref):
    own_ref[...] = keep_ref[0] + got_ref[0]
    send_ref[...] = keep_ref[1] + got_ref[1]


def up_kernel(stores, tensors, _, slot_ref, up_ref, *refs):
    low_refs, out_refs = refs[:tensors], refs[tensors:]
    layers, _, rank, width = up_ref.shape
    low = low_refs[0][...]
    for low_ref in low_refs[1:]:
        low = low + low_ref[...]
    row, column = iota((CAP, CAP * rank), 0), iota((CAP, CAP * rank), 1)
    for k in range(stores):
        for layer in range(layers):
            at = (k * layers + layer) * CAP
            spread = jnp.concatenate([low[at : at + CAP]] * CAP, axis=1)
            spread = jnp.where(row == column // rank, spread, 0.0).astype(BF16)
            chosen = jnp.concatenate(
                [up_ref[layer, slot_ref[k * CAP + c]] for c in range(CAP)], axis=0
            )
            out_refs[k][layer * CAP : (layer + 1) * CAP, :] = jnp.dot(
                spread, chosen, preferred_element_type=F32
            )


def final_kernel(count_ref, pick_ref, own_ref, got_ref, *refs):
    term_refs, out_ref = refs[:-1], refs[-1]
    layers, rows, _ = out_ref.shape
    terms = jnp.concatenate([term_ref[...] for term_ref in term_refs], axis=0)
    pieces = []
    for _ in range(PIECES):
        pieces.append(terms.astype(BF16))
        terms = terms - pieces[-1].astype(F32)
    delta = jnp.dot(
        pick_ref[...], jnp.concatenate(pieces, axis=0), preferred_element_type=F32
    )
    live = iota((rows, 1), 0) < count_ref[0]
    for layer in range(layers):
        total = own_ref[layer] + got_ref[layer] + delta[layer * rows : (layer + 1) * rows]
        out_ref[layer] = jnp.where(live, total, 0.0).astype(BF16)


def params(limit=SMALL):
    return pltpu.CompilerParams(vmem_limit_bytes=limit)


def cost(microseconds):
    return pl.CostEstimate(
        flops=int(microseconds * 1.1535e9), bytes_accessed=0, transcendentals=0
    )


def local(stores, tensors, x, w, down, up, owner, slot, count):
    layers, rows, depth = x.shape
    adapters, rank, width = up.shape[1:]
    half = depth // HALVES
    block = layers * HALVES * CAP
    owner_row = owner.reshape(1, rows)
    slot_row = slot.reshape(1, rows)
    down = pltpu.with_memory_space_constraint(jnp.swapaxes(down, 2, 3), pltpu.HBM)

    def swap(value, axis, size, by):
        if by == 0:
            return value
        return lax.ppermute(value, axis, [(i, i ^ by) for i in range(size)])

    *payloads, pick = pl.pallas_call(
        functools.partial(prepare_kernel, stores),
        out_shape=[jax.ShapeDtypeStruct((block, half + LANES), BF16)] * stores
        + [
            jax.ShapeDtypeStruct((layers * rows, PIECES * stores * layers * CAP), BF16),
        ],
        in_specs=[ANY] * 3,
        out_specs=[VMEM] * (stores + 1),
        scratch_shapes=[
            pltpu.VMEM((1, rows), jnp.int32),
            pltpu.VMEM((1, rows), jnp.int32),
            pltpu.VMEM(x.shape, BF16),
            pltpu.SemaphoreType.DMA((3,)),
        ],
        compiler_params=params(),
        cost_estimate=cost(6),
        name="prepare",
    )(*(pltpu.with_memory_space_constraint(v, pltpu.HBM) for v in (owner_row, slot_row, x)))
    order = [0] + list(range(stores - 1, 0, -1))
    early = min(2, stores)
    blocks = [swap(payloads[k], "store", stores, k) for k in order]

    keep, send, chosen = pl.pallas_call(
        functools.partial(base_kernel, tensors, early),
        out_shape=[jax.ShapeDtypeStruct((tensors // 2, layers, rows, width), F32)] * 2
        + [jax.ShapeDtypeStruct((early, layers, CAP * rank, depth), BF16)],
        in_specs=[HBM] + [VMEM] * (2 + early),
        out_specs=[VMEM] * 3,
        scratch_shapes=[pltpu.SemaphoreType.DMA((early, layers, CAP))],
        compiler_params=params(),
        cost_estimate=cost(6),
        name="base",
    )(down, x, w, *blocks[:early])
    got = swap(send, "tensor", tensors, 1)
    bit = 2
    while keep.shape[0] > 2:
        total, middle = keep + got, keep.shape[0] // 2
        keep, got = total[:middle], swap(total[middle:], "tensor", tensors, bit)
        bit *= 2

    low, slots = pl.pallas_call(
        functools.partial(down_kernel, order, early),
        out_shape=[
            jax.ShapeDtypeStruct((stores * layers * CAP, rank), F32),
            jax.ShapeDtypeStruct((stores * CAP,), jnp.int32),
        ],
        in_specs=[HBM] + [VMEM] * (1 + stores),
        out_specs=[VMEM, SMEM],
        scratch_shapes=[
            pltpu.VMEM((stores - early, layers, CAP * rank, depth), BF16),
            pltpu.SemaphoreType.DMA((stores - early, layers, CAP)),
        ],
        compiler_params=params(LARGE),
        cost_estimate=cost(4),
        name="down",
    )(down, chosen, *blocks)
    lows = [swap(low, "tensor", tensors, j) for j in range(tensors)]
    own, send = pl.pallas_call(
        pair_kernel,
        out_shape=[jax.ShapeDtypeStruct((layers, rows, width), F32)] * 2,
        in_specs=[ANY] + [VMEM] * 2,
        out_specs=[VMEM] * 2,
        compiler_params=params(),
        cost_estimate=cost(0.3),
        name="pair",
    )(low, keep, got)
    got = swap(send, "tensor", tensors, bit)

    terms = pl.pallas_call(
        functools.partial(up_kernel, stores, tensors),
        out_shape=[jax.ShapeDtypeStruct((layers * CAP, width), F32)] * stores,
        in_specs=[ANY, SMEM] + [VMEM] * (1 + tensors),
        out_specs=[VMEM] * stores,
        compiler_params=params(),
        cost_estimate=cost(1),
        name="up",
    )(own, slots, up, *lows)
    returned = [swap(terms[k], "store", stores, k) for k in range(stores)]

    return pl.pallas_call(
        final_kernel,
        out_shape=jax.ShapeDtypeStruct((layers, rows, width), BF16),
        in_specs=[SMEM] + [VMEM] * (3 + stores),
        out_specs=VMEM,
        compiler_params=params(),
        cost_estimate=cost(1),
        name="final",
    )(count, pick, own, got, *returned)


def solution(mesh):
    return jax.shard_map(
        functools.partial(local, mesh.shape["store"], mesh.shape["tensor"]),
        mesh=mesh,
        in_specs=(
            P(None, ("groups", "store"), "tensor"),
            P(None, "tensor", None),
            P(None, "store", "tensor", None),
            P(None, "store", None, "tensor"),
            P(("groups", "store"), None),
            P(("groups", "store")),
            P(("groups", "store")),
        ),
        out_specs=P(None, ("groups", "store"), "tensor"),
        check_vma=False,
    )
```

```python
import functools

import jax
import jax.numpy as jnp
from jax import lax
from jax.experimental import pallas as pl
from jax.experimental.pallas import tpu as pltpu
from jax.sharding import PartitionSpec as P

CAP = 4
HALVES = 2
LANES = 128
F32 = jnp.float32
BF16 = jnp.bfloat16
VMEM = pl.BlockSpec(memory_space=pltpu.VMEM)
SMEM = pl.BlockSpec(memory_space=pltpu.SMEM)
HBM = pl.BlockSpec(memory_space=pltpu.HBM)
ANY = pl.BlockSpec(memory_space=pl.ANY)
SMALL = 8 * 1024 * 1024
LARGE = 24 * 1024 * 1024


def iota(shape, axis):
    return lax.broadcasted_iota(jnp.int32, shape, axis)


def ranks(owner_row):
    rows = owner_row.shape[1]
    down, across = iota((rows, rows), 0), iota((rows, rows), 1)
    owner_row = (owner_row ^ lax.axis_index("store")).astype(F32)
    spread = jnp.broadcast_to(owner_row, (rows, rows))
    owner_col = jnp.sum(jnp.where(down == across, spread, 0.0), axis=1, keepdims=True)
    same = owner_col == spread
    rank_row = jnp.sum(jnp.where(same & (down < across), 1.0, 0.0), axis=0, keepdims=True)
    rank_col = jnp.sum(jnp.where(same & (across < down), 1.0, 0.0), axis=1, keepdims=True)
    return owner_row, rank_row, owner_col, rank_col


def prepare_kernel(back, owner_hbm, slot_hbm, x_hbm, *refs):
    stores = len(back)
    out_refs, (pick_ref, owner_ref, slot_ref, x_ref, sems) = refs[:stores], refs[stores:]
    pairs = ((owner_hbm, owner_ref), (slot_hbm, slot_ref), (x_hbm, x_ref))
    copies = [
        pltpu.make_async_copy(source, target, sems.at[i]) for i, (source, target) in enumerate(pairs)
    ]
    for copy in copies:
        copy.start()
    for copy in copies:
        copy.wait()
    layers, rows, depth = x_ref.shape
    half = depth // HALVES
    block = layers * HALVES * CAP
    hop_row, rank_row, hop_col, rank_col = ranks(owner_ref[...])
    place = hop_row * block + rank_row
    places = jnp.concatenate([place + CAP * part for part in range(layers * HALVES)], axis=1)
    pick = iota((stores * block, layers * HALVES * rows), 0).astype(F32) == places
    stacked = jnp.concatenate(
        [
            x_ref[layer, :, part * half : (part + 1) * half]
            for layer in range(layers)
            for part in range(HALVES)
        ],
        axis=0,
    )
    sent = jnp.dot(pick.astype(BF16), stacked, preferred_element_type=F32).astype(BF16)
    first = iota((stores * block, rows), 0).astype(F32) == place
    slots = jnp.sum(
        jnp.where(first, jnp.broadcast_to(slot_ref[...].astype(F32), first.shape), 0.0),
        axis=1,
        keepdims=True,
    )
    slots = jnp.broadcast_to(slots, (stores * block, LANES)).astype(BF16)
    for k, out_ref in enumerate(out_refs):
        out_ref[:, :half] = sent[k * block : (k + 1) * block]
        out_ref[:, half:] = slots[k * block : (k + 1) * block]
    spots = iota((rows, pick_ref.shape[1]), 1).astype(F32)
    spot = sum(jnp.where(hop_col == float(k), float(i), 0.0) for i, k in enumerate(back))
    place = spot * (layers * CAP) + rank_col
    for layer in range(layers):
        pick_ref[layer * rows : (layer + 1) * rows] = (spots == place + layer * CAP).astype(BF16)


def chunk_order(tensors):
    if tensors == 1:
        return [0]
    rest = [2 * mask for mask in chunk_order(tensors // 2)]
    return rest + [mask + 1 for mask in rest]


def main_kernel(order, tensors, down_hbm, up_hbm, x_ref, w_ref, *refs):
    stores = len(order)
    block_refs, refs = refs[:stores], refs[stores:]
    keep_ref, send_ref, low_ref, up_ref, refs = *refs[:4], refs[4:]
    slot_vmem, slot_smem, chosen_ref, slot_sem, down_sems, up_sems = refs
    layers, _, rank, depth = down_hbm.shape
    half = depth // HALVES
    block = layers * HALVES * CAP
    for i in range(stores):
        tail = block_refs[i][:, half:].astype(F32)
        slot_vmem[i * 8 : (i + 1) * 8] = tail[:8].astype(jnp.int32)
    slot_copy = pltpu.make_async_copy(slot_vmem, slot_smem, slot_sem)
    slot_copy.start()
    slot_copy.wait()

    def fetches(store_hbm, target_ref, sems, i):
        return [
            pltpu.make_async_copy(
                store_hbm.at[layer, slot_smem[i * 8 + c, 0]],
                target_ref.at[i, layer, pl.ds(c * rank, rank)],
                sems.at[i, layer, c],
            )
            for layer in range(layers)
            for c in range(CAP)
        ]

    downs = [fetches(down_hbm, chosen_ref, down_sems, i) for i in range(stores)]
    ups = [fetches(up_hbm, up_ref, up_sems, i) for i in range(stores)]
    for group in downs + ups:
        for copy in group:
            copy.start()

    me = lax.axis_index("tensor")
    width = keep_ref.shape[3]
    for i, mask in enumerate(chunk_order(tensors)):
        out_ref = keep_ref if i < tensors // 2 else send_ref
        columns = pl.ds(pl.multiple_of((me ^ mask) * width, width), width)
        for layer in range(layers):
            out_ref[i % (tensors // 2), layer] = jnp.dot(
                x_ref[layer], w_ref[layer, :, columns], preferred_element_type=F32
            )

    row, column = iota((CAP * rank, block), 0), iota((CAP * rank, block), 1)
    columns = []
    for i in range(stores):
        for copy in downs[i]:
            copy.wait()
        total = jnp.zeros((rank, block), F32)
        for layer in range(layers):
            for part in range(HALVES):
                product = lax.dot_general(
                    chosen_ref[i, layer, :, part * half : (part + 1) * half],
                    block_refs[i][:, :half],
                    (((1,), (1,)), ((), ())),
                    preferred_element_type=F32,
                )
                mine = column == (layer * HALVES + part) * CAP + row // rank
                product = jnp.where(mine, product, 0.0)
                for c in range(CAP):
                    total = total + product[c * rank : (c + 1) * rank]
        columns.append(total)
    turned = jnp.concatenate(columns, axis=1).T
    for i in range(stores):
        for layer in range(layers):
            at = i * block + layer * HALVES * CAP
            low_ref[(i * layers + layer) * CAP : (i * layers + layer + 1) * CAP] = (
                turned[at : at + CAP] + turned[at + CAP : at + 2 * CAP]
            )
    for group in ups:
        for copy in group:
            copy.wait()


def pair_kernel(_, keep_ref, got_ref, own_ref, send_ref):
    own_ref[...] = keep_ref[0] + got_ref[0]
    send_ref[...] = keep_ref[1] + got_ref[1]


def up_kernel(tensors, _, up_ref, *refs):
    low_refs, out_refs = refs[:tensors], refs[tensors:]
    stores, layers, depth, width = up_ref.shape
    rank = depth // CAP
    half = width // HALVES
    low = low_refs[0][...]
    for low_ref in low_refs[1:]:
        low = low + low_ref[...]
    row, column = iota((CAP, depth), 0), iota((CAP, depth), 1)
    for i in range(stores):
        terms = []
        for layer in range(layers):
            at = (i * layers + layer) * CAP
            spread = jnp.concatenate([low[at : at + CAP]] * CAP, axis=1)
            spread = jnp.where(row == column // rank, spread, 0.0).astype(BF16)
            terms.append(jnp.dot(spread, up_ref[i, layer], preferred_element_type=F32))
        terms = jnp.concatenate(terms, axis=0)
        parts = [terms[:, part * half : (part + 1) * half] for part in range(HALVES)]
        out_refs[i][...] = jnp.concatenate(parts, axis=0).astype(BF16)


def final_kernel(count_ref, pick_ref, own_ref, got_ref, *refs):
    term_refs, out_ref = refs[:-1], refs[-1]
    layers, rows, width = out_ref.shape
    half = width // HALVES
    live = iota((rows, 1), 0) < count_ref[0]
    terms = [term_ref[...].astype(F32) for term_ref in term_refs]
    for part in range(HALVES):
        span = slice(part * half, (part + 1) * half)
        mine = slice(part * layers * CAP, (part + 1) * layers * CAP)
        stacked = jnp.concatenate([term[mine] for term in terms], axis=0).astype(BF16)
        delta = jnp.dot(pick_ref[...], stacked, preferred_element_type=F32)
        for layer in range(layers):
            total = own_ref[layer, :, span] + got_ref[layer, :, span]
            total = total + delta[layer * rows : (layer + 1) * rows]
            out_ref[layer, :, span] = jnp.where(live, total, 0.0).astype(BF16)


def params(limit=SMALL):
    return pltpu.CompilerParams(vmem_limit_bytes=limit)


def cost(microseconds):
    return pl.CostEstimate(
        flops=int(microseconds * 1.1535e9), bytes_accessed=0, transcendentals=0
    )


def local(stores, tensors, x, w, down, up, owner, slot, count):
    layers, rows, depth = x.shape
    adapters, rank, width = up.shape[1:]
    half = depth // HALVES
    block = layers * HALVES * CAP
    owner_row = owner.reshape(1, rows)
    slot_row = slot.reshape(1, rows)
    down = pltpu.with_memory_space_constraint(jnp.swapaxes(down, 2, 3), pltpu.HBM)
    up = pltpu.with_memory_space_constraint(up, pltpu.HBM)

    def swap(value, axis, size, by):
        if by == 0:
            return value
        return lax.ppermute(value, axis, [(i, i ^ by) for i in range(size)])

    order = [0] + list(range(stores - 1, 0, -1))
    back = [0] + order[2:] + order[1:2]
    *payloads, pick = pl.pallas_call(
        functools.partial(prepare_kernel, back),
        out_shape=[jax.ShapeDtypeStruct((block, half + LANES), BF16)] * stores
        + [
            jax.ShapeDtypeStruct((layers * rows, stores * layers * CAP), BF16),
        ],
        in_specs=[ANY] * 3,
        out_specs=[VMEM] * (stores + 1),
        scratch_shapes=[
            pltpu.VMEM((1, rows), jnp.int32),
            pltpu.VMEM((1, rows), jnp.int32),
            pltpu.VMEM(x.shape, BF16),
            pltpu.SemaphoreType.DMA((3,)),
        ],
        compiler_params=params(),
        cost_estimate=cost(6),
        name="prepare",
    )(*(pltpu.with_memory_space_constraint(v, pltpu.HBM) for v in (owner_row, slot_row, x)))
    blocks = [swap(payloads[k], "store", stores, k) for k in order]

    keep, send, low, chosen = pl.pallas_call(
        functools.partial(main_kernel, order, tensors),
        out_shape=[jax.ShapeDtypeStruct((tensors // 2, layers, rows, width), F32)] * 2
        + [
            jax.ShapeDtypeStruct((stores * layers * CAP, rank), F32),
            jax.ShapeDtypeStruct((stores, layers, CAP * rank, width), BF16),
        ],
        in_specs=[HBM] * 2 + [VMEM] * (2 + stores),
        out_specs=[VMEM] * 4,
        scratch_shapes=[
            pltpu.VMEM((stores * 8, LANES), jnp.int32),
            pltpu.SMEM((stores * 8, LANES), jnp.int32),
            pltpu.VMEM((stores, layers, CAP * rank, depth), BF16),
            pltpu.SemaphoreType.DMA,
            pltpu.SemaphoreType.DMA((stores, layers, CAP)),
            pltpu.SemaphoreType.DMA((stores, layers, CAP)),
        ],
        compiler_params=params(LARGE),
        cost_estimate=cost(6),
        name="main",
    )(down, up, x, w, *blocks)
    lows = [low] + [swap(low, "tensor", tensors, j) for j in range(tensors - 1, 0, -1)]
    got = swap(send, "tensor", tensors, 1)
    bit = 2
    while keep.shape[0] > 2:
        total, middle = keep + got, keep.shape[0] // 2
        keep, got = total[:middle], swap(total[middle:], "tensor", tensors, bit)
        bit *= 2

    own, send = pl.pallas_call(
        pair_kernel,
        out_shape=[jax.ShapeDtypeStruct((layers, rows, width), F32)] * 2,
        in_specs=[ANY] + [VMEM] * 2,
        out_specs=[VMEM] * 2,
        compiler_params=params(),
        cost_estimate=cost(0.3),
        name="pair",
    )(low, keep, got)
    got = swap(send, "tensor", tensors, bit)

    terms = pl.pallas_call(
        functools.partial(up_kernel, tensors),
        out_shape=[jax.ShapeDtypeStruct((layers * HALVES * CAP, width // HALVES), BF16)] * stores,
        in_specs=[ANY] + [VMEM] * (1 + tensors),
        out_specs=[VMEM] * stores,
        compiler_params=params(),
        cost_estimate=cost(1),
        name="up",
    )(own, chosen, *lows)
    returned = [swap(terms[order.index(k)], "store", stores, k) for k in back]

    return pl.pallas_call(
        final_kernel,
        out_shape=jax.ShapeDtypeStruct((layers, rows, width), BF16),
        in_specs=[SMEM] + [VMEM] * (3 + stores),
        out_specs=VMEM,
        compiler_params=params(),
        cost_estimate=cost(1),
        name="final",
    )(count, pick, own, got, *returned)


def solution(mesh):
    return jax.shard_map(
        functools.partial(local, mesh.shape["store"], mesh.shape["tensor"]),
        mesh=mesh,
        in_specs=(
            P(None, ("groups", "store"), "tensor"),
            P(None, "tensor", None),
            P(None, "store", "tensor", None),
            P(None, "store", None, "tensor"),
            P(("groups", "store"), None),
            P(("groups", "store")),
            P(("groups", "store")),
        ),
        out_specs=P(None, ("groups", "store"), "tensor"),
        check_vma=False,
    )
```

```python
import functools

import jax
import jax.numpy as jnp
from jax import lax
from jax.experimental import pallas as pl
from jax.experimental.pallas import tpu as pltpu
from jax.sharding import PartitionSpec as P

CAP = 4
HALVES = 2
LANES = 128
F32 = jnp.float32
BF16 = jnp.bfloat16
VMEM = pl.BlockSpec(memory_space=pltpu.VMEM)
SMEM = pl.BlockSpec(memory_space=pltpu.SMEM)
HBM = pl.BlockSpec(memory_space=pltpu.HBM)
ANY = pl.BlockSpec(memory_space=pl.ANY)
SMALL = 8 * 1024 * 1024
LARGE = 24 * 1024 * 1024


def iota(shape, axis):
    return lax.broadcasted_iota(jnp.int32, shape, axis)


def ranks(owner_row):
    rows = owner_row.shape[1]
    down, across = iota((rows, rows), 0), iota((rows, rows), 1)
    owner_row = (owner_row ^ lax.axis_index("store")).astype(F32)
    spread = jnp.broadcast_to(owner_row, (rows, rows))
    owner_col = jnp.sum(jnp.where(down == across, spread, 0.0), axis=1, keepdims=True)
    same = owner_col == spread
    rank_row = jnp.sum(jnp.where(same & (down < across), 1.0, 0.0), axis=0, keepdims=True)
    rank_col = jnp.sum(jnp.where(same & (across < down), 1.0, 0.0), axis=1, keepdims=True)
    return owner_row, rank_row, owner_col, rank_col


def prepare_kernel(back, owner_hbm, slot_hbm, x_hbm, *refs):
    stores = len(back)
    out_refs, (pick_ref, owner_ref, slot_ref, x_ref, sems) = refs[:stores], refs[stores:]
    pairs = ((owner_hbm, owner_ref), (slot_hbm, slot_ref), (x_hbm, x_ref))
    copies = [
        pltpu.make_async_copy(source, target, sems.at[i]) for i, (source, target) in enumerate(pairs)
    ]
    for copy in copies:
        copy.start()
    for copy in copies:
        copy.wait()
    layers, rows, depth = x_ref.shape
    half = depth // HALVES
    block = layers * HALVES * CAP
    hop_row, rank_row, hop_col, rank_col = ranks(owner_ref[...])
    place = hop_row * block + rank_row
    places = jnp.concatenate([place + CAP * part for part in range(layers * HALVES)], axis=1)
    pick = iota((stores * block, layers * HALVES * rows), 0).astype(F32) == places
    stacked = jnp.concatenate(
        [
            x_ref[layer, :, part * half : (part + 1) * half]
            for layer in range(layers)
            for part in range(HALVES)
        ],
        axis=0,
    )
    sent = jnp.dot(pick.astype(BF16), stacked, preferred_element_type=F32).astype(BF16)
    first = iota((stores * block, rows), 0).astype(F32) == place
    slots = jnp.sum(
        jnp.where(first, jnp.broadcast_to(slot_ref[...].astype(F32), first.shape), 0.0),
        axis=1,
        keepdims=True,
    )
    slots = jnp.broadcast_to(slots, (stores * block, LANES)).astype(BF16)
    for k, out_ref in enumerate(out_refs):
        out_ref[:, :half] = sent[k * block : (k + 1) * block]
        out_ref[:, half:] = slots[k * block : (k + 1) * block]
    spots = iota((rows, pick_ref.shape[1]), 1).astype(F32)
    spot = sum(jnp.where(hop_col == float(k), float(i), 0.0) for i, k in enumerate(back))
    place = spot * (layers * CAP) + rank_col
    for layer in range(layers):
        pick_ref[layer * rows : (layer + 1) * rows] = (spots == place + layer * CAP).astype(BF16)


def chunk_order(tensors):
    if tensors == 1:
        return [0]
    rest = [2 * mask for mask in chunk_order(tensors // 2)]
    return rest + [mask + 1 for mask in rest]


def slot_copy(block_refs, half, vmem_ref, smem_ref, sem):
    for i, block_ref in enumerate(block_refs):
        tail = block_ref[:, half:].astype(F32)
        vmem_ref[i * 8 : (i + 1) * 8] = tail[:8].astype(jnp.int32)
    copy = pltpu.make_async_copy(vmem_ref, smem_ref, sem)
    copy.start()
    return copy


def fetches(store_hbm, smem_ref, i, target_ref, sems):
    rank = store_hbm.shape[2]
    return [
        pltpu.make_async_copy(
            store_hbm.at[:, smem_ref[i * 8 + c, 0]],
            target_ref.at[:, pl.ds(c * rank, rank)],
            sems.at[c],
        )
        for c in range(CAP)
    ]


def start_some(waiting, count):
    for copy in waiting[:count]:
        copy.start()
    del waiting[:count]


def base_kernel(tensors, early, down_hbm, x_ref, w_ref, *refs):
    block_refs, refs = refs[:early], refs[early:]
    keep_ref, send_ref, chosen_ref, slot_vmem, slot_smem, slot_sem, sems = refs
    layers, _, depth = x_ref.shape
    width = keep_ref.shape[3]
    slots = slot_copy(block_refs, depth // HALVES, slot_vmem, slot_smem, slot_sem)
    me = lax.axis_index("tensor")
    copies, waiting = [], []
    for i, mask in enumerate(chunk_order(tensors)):
        out_ref = keep_ref if i < tensors // 2 else send_ref
        columns = pl.ds(pl.multiple_of((me ^ mask) * width, width), width)
        for layer in range(layers):
            out_ref[i % (tensors // 2), layer] = jnp.dot(
                x_ref[layer], w_ref[layer, :, columns], preferred_element_type=F32
            )
            if not copies:
                slots.wait()
                for j in range(early):
                    copies += fetches(down_hbm, slot_smem, j, chosen_ref.at[j], sems.at[j])
                waiting = list(copies)
            start_some(waiting, 2)
    start_some(waiting, len(waiting))
    for copy in copies:
        copy.wait()


def down_kernel(early, down_hbm, up_hbm, early_ref, *refs):
    stores = len(refs) - 9
    block_refs, (low_ref, up_ref, late_ref, *refs) = refs[:stores], refs[stores:]
    slot_vmem, slot_smem, slot_sem, down_sems, up_sems, kept_ref = refs
    layers, _, rank, depth = down_hbm.shape
    half = depth // HALVES
    block = layers * HALVES * CAP
    slots = slot_copy(block_refs, half, slot_vmem, slot_smem, slot_sem)
    row, column = iota((CAP * rank, block), 0), iota((CAP * rank, block), 1)
    copies, waiting = [], []
    for i in range(stores):
        chosen_ref = early_ref.at[i] if i < early else late_ref.at[i - early]
        if i >= early:
            for copy in copies[i - early]:
                copy.wait()
        total = jnp.zeros((rank, block), F32)
        for layer in range(layers):
            for part in range(HALVES):
                product = lax.dot_general(
                    chosen_ref[layer, :, part * half : (part + 1) * half],
                    block_refs[i][:, :half],
                    (((1,), (1,)), ((), ())),
                    preferred_element_type=F32,
                )
                mine = column == (layer * HALVES + part) * CAP + row // rank
                product = jnp.where(mine, product, 0.0)
                for c in range(CAP):
                    total = total + product[c * rank : (c + 1) * rank]
                if not copies:
                    slots.wait()
                    for j in range(early, stores):
                        at = j - early
                        copies.append(
                            fetches(down_hbm, slot_smem, j, late_ref.at[at], down_sems.at[at])
                        )
                    ups = [
                        fetches(up_hbm, slot_smem, j, up_ref.at[j], up_sems.at[j])
                        for j in range(stores)
                    ]
                    waiting = sum(copies + ups, [])
                start_some(waiting, 2)
        kept_ref[:, i * block : (i + 1) * block] = total
    start_some(waiting, len(waiting))
    turned = kept_ref[...].T
    for i in range(stores):
        for layer in range(layers):
            at = i * block + layer * HALVES * CAP
            low_ref[(i * layers + layer) * CAP : (i * layers + layer + 1) * CAP] = (
                turned[at : at + CAP] + turned[at + CAP : at + 2 * CAP]
            )
    for group in ups:
        for copy in group:
            copy.wait()


def pair_kernel(_, keep_ref, got_ref, own_ref, send_ref):
    own_ref[...] = keep_ref[0] + got_ref[0]
    send_ref[...] = keep_ref[1] + got_ref[1]


def up_kernel(tensors, _, up_ref, *refs):
    low_refs, out_refs = refs[:tensors], refs[tensors:]
    stores, layers, depth, width = up_ref.shape
    rank = depth // CAP
    half = width // HALVES
    low = low_refs[0][...]
    for low_ref in low_refs[1:]:
        low = low + low_ref[...]
    row, column = iota((CAP, depth), 0), iota((CAP, depth), 1)
    for i in range(stores):
        terms = []
        for layer in range(layers):
            at = (i * layers + layer) * CAP
            spread = jnp.concatenate([low[at : at + CAP]] * CAP, axis=1)
            spread = jnp.where(row == column // rank, spread, 0.0).astype(BF16)
            terms.append(jnp.dot(spread, up_ref[i, layer], preferred_element_type=F32))
        terms = jnp.concatenate(terms, axis=0)
        parts = [terms[:, part * half : (part + 1) * half] for part in range(HALVES)]
        out_refs[i][...] = jnp.concatenate(parts, axis=0).astype(BF16)


def final_kernel(count_ref, pick_ref, own_ref, got_ref, *refs):
    term_refs, out_ref = refs[:-1], refs[-1]
    layers, rows, width = out_ref.shape
    half = width // HALVES
    live = iota((rows, 1), 0) < count_ref[0]
    terms = [term_ref[...].astype(F32) for term_ref in term_refs]
    for part in range(HALVES):
        span = slice(part * half, (part + 1) * half)
        mine = slice(part * layers * CAP, (part + 1) * layers * CAP)
        stacked = jnp.concatenate([term[mine] for term in terms], axis=0).astype(BF16)
        delta = jnp.dot(pick_ref[...], stacked, preferred_element_type=F32)
        for layer in range(layers):
            total = own_ref[layer, :, span] + got_ref[layer, :, span]
            total = total + delta[layer * rows : (layer + 1) * rows]
            out_ref[layer, :, span] = jnp.where(live, total, 0.0).astype(BF16)


def params(limit=SMALL):
    return pltpu.CompilerParams(vmem_limit_bytes=limit)


def cost(microseconds):
    return pl.CostEstimate(
        flops=int(microseconds * 1.1535e9), bytes_accessed=0, transcendentals=0
    )


def local(stores, tensors, x, w, down, up, owner, slot, count):
    layers, rows, depth = x.shape
    adapters, rank, width = up.shape[1:]
    half = depth // HALVES
    block = layers * HALVES * CAP
    owner_row = owner.reshape(1, rows)
    slot_row = slot.reshape(1, rows)
    down = pltpu.with_memory_space_constraint(jnp.swapaxes(down, 2, 3), pltpu.HBM)
    up = pltpu.with_memory_space_constraint(up, pltpu.HBM)

    def swap(value, axis, size, by):
        if by == 0:
            return value
        return lax.ppermute(value, axis, [(i, i ^ by) for i in range(size)])

    order = [0] + list(range(stores - 1, 0, -1))
    back = [0] + order[2:] + order[1:2]
    *payloads, pick = pl.pallas_call(
        functools.partial(prepare_kernel, back),
        out_shape=[jax.ShapeDtypeStruct((block, half + LANES), BF16)] * stores
        + [
            jax.ShapeDtypeStruct((layers * rows, stores * layers * CAP), BF16),
        ],
        in_specs=[ANY] * 3,
        out_specs=[VMEM] * (stores + 1),
        scratch_shapes=[
            pltpu.VMEM((1, rows), jnp.int32),
            pltpu.VMEM((1, rows), jnp.int32),
            pltpu.VMEM(x.shape, BF16),
            pltpu.SemaphoreType.DMA((3,)),
        ],
        compiler_params=params(),
        cost_estimate=cost(6),
        name="prepare",
    )(*(pltpu.with_memory_space_constraint(v, pltpu.HBM) for v in (owner_row, slot_row, x)))
    blocks = [swap(payloads[k], "store", stores, k) for k in order]

    early = min(2, stores)
    keep, send, chosen = pl.pallas_call(
        functools.partial(base_kernel, tensors, early),
        out_shape=[jax.ShapeDtypeStruct((tensors // 2, layers, rows, width), F32)] * 2
        + [jax.ShapeDtypeStruct((early, layers, CAP * rank, depth), BF16)],
        in_specs=[HBM] + [VMEM] * (2 + early),
        out_specs=[VMEM] * 3,
        scratch_shapes=[
            pltpu.VMEM((early * 8, LANES), jnp.int32),
            pltpu.SMEM((early * 8, LANES), jnp.int32),
            pltpu.SemaphoreType.DMA,
            pltpu.SemaphoreType.DMA((early, CAP)),
        ],
        compiler_params=params(),
        cost_estimate=cost(6),
        name="base",
    )(down, x, w, *blocks[:early])

    low, chosen = pl.pallas_call(
        functools.partial(down_kernel, early),
        out_shape=[
            jax.ShapeDtypeStruct((stores * layers * CAP, rank), F32),
            jax.ShapeDtypeStruct((stores, layers, CAP * rank, width), BF16),
        ],
        in_specs=[HBM] * 2 + [VMEM] * (1 + stores),
        out_specs=[VMEM] * 2,
        scratch_shapes=[
            pltpu.VMEM((stores - early, layers, CAP * rank, depth), BF16),
            pltpu.VMEM((stores * 8, LANES), jnp.int32),
            pltpu.SMEM((stores * 8, LANES), jnp.int32),
            pltpu.SemaphoreType.DMA,
            pltpu.SemaphoreType.DMA((stores - early, CAP)),
            pltpu.SemaphoreType.DMA((stores, CAP)),
            pltpu.VMEM((rank, stores * block), F32),
        ],
        compiler_params=params(LARGE),
        cost_estimate=cost(4),
        name="down",
    )(down, up, chosen, *blocks)
    lows = [low] + [swap(low, "tensor", tensors, j) for j in range(tensors - 1, 0, -1)]
    got = swap(send, "tensor", tensors, 1)
    bit = 2
    while keep.shape[0] > 2:
        total, middle = keep + got, keep.shape[0] // 2
        keep, got = total[:middle], swap(total[middle:], "tensor", tensors, bit)
        bit *= 2

    own, send = pl.pallas_call(
        pair_kernel,
        out_shape=[jax.ShapeDtypeStruct((layers, rows, width), F32)] * 2,
        in_specs=[ANY] + [VMEM] * 2,
        out_specs=[VMEM] * 2,
        compiler_params=params(),
        cost_estimate=cost(0.3),
        name="pair",
    )(low, keep, got)
    got = swap(send, "tensor", tensors, bit)

    terms = pl.pallas_call(
        functools.partial(up_kernel, tensors),
        out_shape=[jax.ShapeDtypeStruct((layers * HALVES * CAP, width // HALVES), BF16)] * stores,
        in_specs=[ANY] + [VMEM] * (1 + tensors),
        out_specs=[VMEM] * stores,
        compiler_params=params(),
        cost_estimate=cost(1),
        name="up",
    )(own, chosen, *lows)
    returned = [swap(terms[order.index(k)], "store", stores, k) for k in back]

    return pl.pallas_call(
        final_kernel,
        out_shape=jax.ShapeDtypeStruct((layers, rows, width), BF16),
        in_specs=[SMEM] + [VMEM] * (3 + stores),
        out_specs=VMEM,
        compiler_params=params(),
        cost_estimate=cost(1),
        name="final",
    )(count, pick, own, got, *returned)


def solution(mesh):
    return jax.shard_map(
        functools.partial(local, mesh.shape["store"], mesh.shape["tensor"]),
        mesh=mesh,
        in_specs=(
            P(None, ("groups", "store"), "tensor"),
            P(None, "tensor", None),
            P(None, "store", "tensor", None),
            P(None, "store", None, "tensor"),
            P(("groups", "store"), None),
            P(("groups", "store")),
            P(("groups", "store")),
        ),
        out_specs=P(None, ("groups", "store"), "tensor"),
        check_vma=False,
    )
```

```python
import functools

import jax
import jax.numpy as jnp
from jax import lax
from jax.experimental import pallas as pl
from jax.experimental.pallas import tpu as pltpu
from jax.sharding import PartitionSpec as P

CAP = 4
HALVES = 2
LANES = 128
F32 = jnp.float32
BF16 = jnp.bfloat16
VMEM = pl.BlockSpec(memory_space=pltpu.VMEM)
SMEM = pl.BlockSpec(memory_space=pltpu.SMEM)
HBM = pl.BlockSpec(memory_space=pltpu.HBM)
ANY = pl.BlockSpec(memory_space=pl.ANY)
SMALL = 8 * 1024 * 1024
LARGE = 24 * 1024 * 1024


def iota(shape, axis):
    return lax.broadcasted_iota(jnp.int32, shape, axis)


def ranks(owner_row):
    rows = owner_row.shape[1]
    down, across = iota((rows, rows), 0), iota((rows, rows), 1)
    owner_row = (owner_row ^ lax.axis_index("store")).astype(F32)
    spread = jnp.broadcast_to(owner_row, (rows, rows))
    owner_col = jnp.sum(jnp.where(down == across, spread, 0.0), axis=1, keepdims=True)
    same = owner_col == spread
    rank_row = jnp.sum(jnp.where(same & (down < across), 1.0, 0.0), axis=0, keepdims=True)
    rank_col = jnp.sum(jnp.where(same & (across < down), 1.0, 0.0), axis=1, keepdims=True)
    return owner_row, rank_row, owner_col, rank_col


def prepare_kernel(back, owner_hbm, slot_hbm, x_hbm, *refs):
    stores = len(back)
    out_refs, (pick_ref, owner_ref, slot_ref, x_ref, sems) = refs[:stores], refs[stores:]
    pairs = ((owner_hbm, owner_ref), (slot_hbm, slot_ref), (x_hbm, x_ref))
    copies = [
        pltpu.make_async_copy(source, target, sems.at[i]) for i, (source, target) in enumerate(pairs)
    ]
    for copy in copies:
        copy.start()
    for copy in copies:
        copy.wait()
    layers, rows, depth = x_ref.shape
    half = depth // HALVES
    block = layers * HALVES * CAP
    hop_row, rank_row, hop_col, rank_col = ranks(owner_ref[...])
    place = hop_row * block + rank_row
    places = jnp.concatenate([place + CAP * part for part in range(layers * HALVES)], axis=1)
    pick = iota((stores * block, layers * HALVES * rows), 0).astype(F32) == places
    stacked = jnp.concatenate(
        [
            x_ref[layer, :, part * half : (part + 1) * half]
            for layer in range(layers)
            for part in range(HALVES)
        ],
        axis=0,
    )
    sent = jnp.dot(pick.astype(BF16), stacked, preferred_element_type=F32).astype(BF16)
    first = iota((stores * block, rows), 0).astype(F32) == place
    slots = jnp.sum(
        jnp.where(first, jnp.broadcast_to(slot_ref[...].astype(F32), first.shape), 0.0),
        axis=1,
        keepdims=True,
    )
    slots = jnp.broadcast_to(slots, (stores * block, LANES)).astype(BF16)
    for k, out_ref in enumerate(out_refs):
        out_ref[:, :half] = sent[k * block : (k + 1) * block]
        out_ref[:, half:] = slots[k * block : (k + 1) * block]
    spots = iota((rows, pick_ref.shape[1]), 1).astype(F32)
    spot = sum(jnp.where(hop_col == float(k), float(i), 0.0) for i, k in enumerate(back))
    place = spot * (layers * CAP) + rank_col
    for layer in range(layers):
        pick_ref[layer * rows : (layer + 1) * rows] = (spots == place + layer * CAP).astype(BF16)


def chunk_order(tensors):
    if tensors == 1:
        return [0]
    rest = [2 * mask for mask in chunk_order(tensors // 2)]
    return rest + [mask + 1 for mask in rest]


def slot_copy(block_refs, half, vmem_ref, smem_ref, sem):
    for i, block_ref in enumerate(block_refs):
        tail = block_ref[:, half:].astype(F32)
        vmem_ref[i * 8 : (i + 1) * 8] = tail[:8].astype(jnp.int32)
    copy = pltpu.make_async_copy(vmem_ref, smem_ref, sem)
    copy.start()
    return copy


def fetch(store_hbm, slot, target_ref, sem, c):
    rank = store_hbm.shape[2]
    return pltpu.make_async_copy(
        store_hbm.at[:, slot], target_ref.at[:, pl.ds(pl.multiple_of(c * rank, rank), rank)], sem
    )


def each_slot(body):
    def step(c, carry):
        body(c)
        return carry

    lax.fori_loop(0, CAP, step, 0)


def base_kernel(tensors, early, down_hbm, x_ref, w_ref, *refs):
    block_refs, refs = refs[:early], refs[early:]
    keep_ref, send_ref, chosen_ref, slot_vmem, slot_smem, slot_sem, sems = refs
    layers, _, depth = x_ref.shape
    width = keep_ref.shape[3]
    slots = slot_copy(block_refs, depth // HALVES, slot_vmem, slot_smem, slot_sem)
    slots.wait()

    def copy(i, c):
        slot = slot_smem[i * 8 + c, 0]
        return fetch(down_hbm, slot, chosen_ref.at[i], sems.at[i, c], c)

    for i in range(early):
        each_slot(lambda c, i=i: copy(i, c).start())
    me = lax.axis_index("tensor")
    for i, mask in enumerate(chunk_order(tensors)):
        out_ref = keep_ref if i < tensors // 2 else send_ref
        columns = pl.ds(pl.multiple_of((me ^ mask) * width, width), width)
        for layer in range(layers):
            out_ref[i % (tensors // 2), layer] = jnp.dot(
                x_ref[layer], w_ref[layer, :, columns], preferred_element_type=F32
            )
    for i in range(early):
        each_slot(lambda c, i=i: copy(i, c).wait())


def down_kernel(early, down_hbm, up_hbm, early_ref, *refs):
    stores = len(refs) - 9
    block_refs, (low_ref, up_ref, late_ref, *refs) = refs[:stores], refs[stores:]
    slot_vmem, slot_smem, slot_sem, down_sems, up_sems, kept_ref = refs
    layers, _, rank, depth = down_hbm.shape
    half = depth // HALVES
    block = layers * HALVES * CAP
    slots = slot_copy(block_refs, half, slot_vmem, slot_smem, slot_sem)
    slots.wait()

    def copy_down(i, c):
        target_ref = late_ref.at[i - early]
        return fetch(down_hbm, slot_smem[i * 8 + c, 0], target_ref, down_sems.at[i - early, c], c)

    def copy_up(i, c):
        return fetch(up_hbm, slot_smem[i * 8 + c, 0], up_ref.at[i], up_sems.at[i, c], c)

    for i in range(early, stores):
        each_slot(lambda c, i=i: copy_down(i, c).start())
    for i in range(stores):
        each_slot(lambda c, i=i: copy_up(i, c).start())
    row, column = iota((CAP * rank, block), 0), iota((CAP * rank, block), 1)
    for i in range(stores):
        chosen_ref = early_ref.at[i] if i < early else late_ref.at[i - early]
        if i >= early:
            each_slot(lambda c, i=i: copy_down(i, c).wait())
        total = jnp.zeros((rank, block), F32)
        for layer in range(layers):
            for part in range(HALVES):
                product = lax.dot_general(
                    chosen_ref[layer, :, part * half : (part + 1) * half],
                    block_refs[i][:, :half],
                    (((1,), (1,)), ((), ())),
                    preferred_element_type=F32,
                )
                mine = column == (layer * HALVES + part) * CAP + row // rank
                product = jnp.where(mine, product, 0.0)
                for c in range(CAP):
                    total = total + product[c * rank : (c + 1) * rank]
        kept_ref[:, i * block : (i + 1) * block] = total
    turned = kept_ref[...].T
    for i in range(stores):
        for layer in range(layers):
            at = i * block + layer * HALVES * CAP
            low_ref[(i * layers + layer) * CAP : (i * layers + layer + 1) * CAP] = (
                turned[at : at + CAP] + turned[at + CAP : at + 2 * CAP]
            )
    for i in range(stores):
        each_slot(lambda c, i=i: copy_up(i, c).wait())


def pair_kernel(_, keep_ref, got_ref, own_ref, send_ref):
    own_ref[...] = keep_ref[0] + got_ref[0]
    send_ref[...] = keep_ref[1] + got_ref[1]


def up_kernel(tensors, _, up_ref, *refs):
    low_refs, out_refs = refs[:tensors], refs[tensors:]
    stores, layers, depth, width = up_ref.shape
    rank = depth // CAP
    half = width // HALVES
    low = low_refs[0][...]
    for low_ref in low_refs[1:]:
        low = low + low_ref[...]
    row, column = iota((CAP, depth), 0), iota((CAP, depth), 1)
    for i in range(stores):
        terms = []
        for layer in range(layers):
            at = (i * layers + layer) * CAP
            spread = jnp.concatenate([low[at : at + CAP]] * CAP, axis=1)
            spread = jnp.where(row == column // rank, spread, 0.0).astype(BF16)
            terms.append(jnp.dot(spread, up_ref[i, layer], preferred_element_type=F32))
        terms = jnp.concatenate(terms, axis=0)
        parts = [terms[:, part * half : (part + 1) * half] for part in range(HALVES)]
        out_refs[i][...] = jnp.concatenate(parts, axis=0).astype(BF16)


def final_kernel(count_ref, pick_ref, own_ref, got_ref, *refs):
    term_refs, out_ref = refs[:-1], refs[-1]
    layers, rows, width = out_ref.shape
    half = width // HALVES
    live = iota((rows, 1), 0) < count_ref[0]
    terms = [term_ref[...].astype(F32) for term_ref in term_refs]
    for part in range(HALVES):
        span = slice(part * half, (part + 1) * half)
        mine = slice(part * layers * CAP, (part + 1) * layers * CAP)
        stacked = jnp.concatenate([term[mine] for term in terms], axis=0).astype(BF16)
        delta = jnp.dot(pick_ref[...], stacked, preferred_element_type=F32)
        for layer in range(layers):
            total = own_ref[layer, :, span] + got_ref[layer, :, span]
            total = total + delta[layer * rows : (layer + 1) * rows]
            out_ref[layer, :, span] = jnp.where(live, total, 0.0).astype(BF16)


def params(limit=SMALL):
    return pltpu.CompilerParams(vmem_limit_bytes=limit)


def cost(microseconds):
    return pl.CostEstimate(
        flops=int(microseconds * 1.1535e9), bytes_accessed=0, transcendentals=0
    )


def local(stores, tensors, x, w, down, up, owner, slot, count):
    layers, rows, depth = x.shape
    adapters, rank, width = up.shape[1:]
    half = depth // HALVES
    block = layers * HALVES * CAP
    owner_row = owner.reshape(1, rows)
    slot_row = slot.reshape(1, rows)
    down = pltpu.with_memory_space_constraint(jnp.swapaxes(down, 2, 3), pltpu.HBM)
    up = pltpu.with_memory_space_constraint(up, pltpu.HBM)

    def swap(value, axis, size, by):
        if by == 0:
            return value
        return lax.ppermute(value, axis, [(i, i ^ by) for i in range(size)])

    order = [0] + list(range(stores - 1, 0, -1))
    back = [0] + order[2:] + order[1:2]
    *payloads, pick = pl.pallas_call(
        functools.partial(prepare_kernel, back),
        out_shape=[jax.ShapeDtypeStruct((block, half + LANES), BF16)] * stores
        + [
            jax.ShapeDtypeStruct((layers * rows, stores * layers * CAP), BF16),
        ],
        in_specs=[ANY] * 3,
        out_specs=[VMEM] * (stores + 1),
        scratch_shapes=[
            pltpu.VMEM((1, rows), jnp.int32),
            pltpu.VMEM((1, rows), jnp.int32),
            pltpu.VMEM(x.shape, BF16),
            pltpu.SemaphoreType.DMA((3,)),
        ],
        compiler_params=params(),
        cost_estimate=cost(6),
        name="prepare",
    )(*(pltpu.with_memory_space_constraint(v, pltpu.HBM) for v in (owner_row, slot_row, x)))
    blocks = [swap(payloads[k], "store", stores, k) for k in order]

    early = min(2, stores)
    keep, send, chosen = pl.pallas_call(
        functools.partial(base_kernel, tensors, early),
        out_shape=[jax.ShapeDtypeStruct((tensors // 2, layers, rows, width), F32)] * 2
        + [jax.ShapeDtypeStruct((early, layers, CAP * rank, depth), BF16)],
        in_specs=[HBM] + [VMEM] * (2 + early),
        out_specs=[VMEM] * 3,
        scratch_shapes=[
            pltpu.VMEM((early * 8, LANES), jnp.int32),
            pltpu.SMEM((early * 8, LANES), jnp.int32),
            pltpu.SemaphoreType.DMA,
            pltpu.SemaphoreType.DMA((early, CAP)),
        ],
        compiler_params=params(),
        cost_estimate=cost(6),
        name="base",
    )(down, x, w, *blocks[:early])

    low, chosen = pl.pallas_call(
        functools.partial(down_kernel, early),
        out_shape=[
            jax.ShapeDtypeStruct((stores * layers * CAP, rank), F32),
            jax.ShapeDtypeStruct((stores, layers, CAP * rank, width), BF16),
        ],
        in_specs=[HBM] * 2 + [VMEM] * (1 + stores),
        out_specs=[VMEM] * 2,
        scratch_shapes=[
            pltpu.VMEM((stores - early, layers, CAP * rank, depth), BF16),
            pltpu.VMEM((stores * 8, LANES), jnp.int32),
            pltpu.SMEM((stores * 8, LANES), jnp.int32),
            pltpu.SemaphoreType.DMA,
            pltpu.SemaphoreType.DMA((stores - early, CAP)),
            pltpu.SemaphoreType.DMA((stores, CAP)),
            pltpu.VMEM((rank, stores * block), F32),
        ],
        compiler_params=params(LARGE),
        cost_estimate=cost(4),
        name="down",
    )(down, up, chosen, *blocks)
    lows = [low] + [swap(low, "tensor", tensors, j) for j in range(tensors - 1, 0, -1)]
    got = swap(send, "tensor", tensors, 1)
    bit = 2
    while keep.shape[0] > 2:
        total, middle = keep + got, keep.shape[0] // 2
        keep, got = total[:middle], swap(total[middle:], "tensor", tensors, bit)
        bit *= 2

    own, send = pl.pallas_call(
        pair_kernel,
        out_shape=[jax.ShapeDtypeStruct((layers, rows, width), F32)] * 2,
        in_specs=[ANY] + [VMEM] * 2,
        out_specs=[VMEM] * 2,
        compiler_params=params(),
        cost_estimate=cost(0.3),
        name="pair",
    )(low, keep, got)
    got = swap(send, "tensor", tensors, bit)

    terms = pl.pallas_call(
        functools.partial(up_kernel, tensors),
        out_shape=[jax.ShapeDtypeStruct((layers * HALVES * CAP, width // HALVES), BF16)] * stores,
        in_specs=[ANY] + [VMEM] * (1 + tensors),
        out_specs=[VMEM] * stores,
        compiler_params=params(),
        cost_estimate=cost(1),
        name="up",
    )(own, chosen, *lows)
    returned = [swap(terms[order.index(k)], "store", stores, k) for k in back]

    return pl.pallas_call(
        final_kernel,
        out_shape=jax.ShapeDtypeStruct((layers, rows, width), BF16),
        in_specs=[SMEM] + [VMEM] * (3 + stores),
        out_specs=VMEM,
        compiler_params=params(),
        cost_estimate=cost(1),
        name="final",
    )(count, pick, own, got, *returned)


def solution(mesh):
    return jax.shard_map(
        functools.partial(local, mesh.shape["store"], mesh.shape["tensor"]),
        mesh=mesh,
        in_specs=(
            P(None, ("groups", "store"), "tensor"),
            P(None, "tensor", None),
            P(None, "store", "tensor", None),
            P(None, "store", None, "tensor"),
            P(("groups", "store"), None),
            P(("groups", "store")),
            P(("groups", "store")),
        ),
        out_specs=P(None, ("groups", "store"), "tensor"),
        check_vma=False,
    )
```

```python
import functools

import jax
import jax.numpy as jnp
from jax import lax
from jax.experimental import pallas as pl
from jax.experimental.pallas import tpu as pltpu
from jax.sharding import PartitionSpec as P

CAP = 4
HALVES = 2
LANES = 128
F32 = jnp.float32
BF16 = jnp.bfloat16
VMEM = pl.BlockSpec(memory_space=pltpu.VMEM)
SMEM = pl.BlockSpec(memory_space=pltpu.SMEM)
HBM = pl.BlockSpec(memory_space=pltpu.HBM)
ANY = pl.BlockSpec(memory_space=pl.ANY)
SMALL = 8 * 1024 * 1024
LARGE = 24 * 1024 * 1024


def iota(shape, axis):
    return lax.broadcasted_iota(jnp.int32, shape, axis)


def ranks(owner_row):
    rows = owner_row.shape[1]
    down, across = iota((rows, rows), 0), iota((rows, rows), 1)
    owner_row = (owner_row ^ lax.axis_index("store")).astype(F32)
    spread = jnp.broadcast_to(owner_row, (rows, rows))
    owner_col = jnp.sum(jnp.where(down == across, spread, 0.0), axis=1, keepdims=True)
    same = owner_col == spread
    rank_row = jnp.sum(jnp.where(same & (down < across), 1.0, 0.0), axis=0, keepdims=True)
    rank_col = jnp.sum(jnp.where(same & (across < down), 1.0, 0.0), axis=1, keepdims=True)
    return owner_row, rank_row, owner_col, rank_col


def prepare_kernel(back, owner_hbm, slot_hbm, x_hbm, *refs):
    stores = len(back)
    out_refs, (pick_ref, owner_ref, slot_ref, x_ref, sems) = refs[:stores], refs[stores:]
    pairs = ((owner_hbm, owner_ref), (slot_hbm, slot_ref), (x_hbm, x_ref))
    copies = [
        pltpu.make_async_copy(source, target, sems.at[i]) for i, (source, target) in enumerate(pairs)
    ]
    for copy in copies:
        copy.start()
    for copy in copies[:2]:
        copy.wait()
    layers, rows, depth = x_ref.shape
    half = depth // HALVES
    block = layers * HALVES * CAP
    hop_row, rank_row, hop_col, rank_col = ranks(owner_ref[...])
    place = hop_row * block + rank_row
    places = jnp.concatenate([place + CAP * part for part in range(layers * HALVES)], axis=1)
    pick = iota((stores * block, layers * HALVES * rows), 0).astype(F32) == places
    spots = iota((rows, pick_ref.shape[1]), 1).astype(F32)
    spot = sum(jnp.where(hop_col == float(k), float(i), 0.0) for i, k in enumerate(back))
    back_place = spot * (layers * CAP) + rank_col
    for layer in range(layers):
        pick_ref[layer * rows : (layer + 1) * rows] = (spots == back_place + layer * CAP).astype(BF16)
    copies[2].wait()
    stacked = jnp.concatenate(
        [
            x_ref[layer, :, part * half : (part + 1) * half]
            for layer in range(layers)
            for part in range(HALVES)
        ],
        axis=0,
    )
    sent = jnp.dot(pick.astype(BF16), stacked, preferred_element_type=F32).astype(BF16)
    first = iota((stores * block, rows), 0).astype(F32) == place
    slots = jnp.sum(
        jnp.where(first, jnp.broadcast_to(slot_ref[...].astype(F32), first.shape), 0.0),
        axis=1,
        keepdims=True,
    )
    slots = jnp.broadcast_to(slots, (stores * block, LANES)).astype(BF16)
    for k, out_ref in enumerate(out_refs):
        out_ref[:, :half] = sent[k * block : (k + 1) * block]
        out_ref[:, half:] = slots[k * block : (k + 1) * block]


def chunk_order(tensors):
    if tensors == 1:
        return [0]
    rest = [2 * mask for mask in chunk_order(tensors // 2)]
    return rest + [mask + 1 for mask in rest]


def read_slots(block_refs, half, slot_ref):
    for i, block_ref in enumerate(block_refs):
        tail = block_ref[:, half:].astype(F32)
        for c in range(CAP):
            slot_ref[i * CAP + c] = tail[c, 0].astype(jnp.int32)


def fetch(store_hbm, slot, target_ref, sem, c):
    rank = store_hbm.shape[2]
    return pltpu.make_async_copy(
        store_hbm.at[:, slot], target_ref.at[:, pl.ds(pl.multiple_of(c * rank, rank), rank)], sem
    )


def each_slot(body):
    def step(c, carry):
        body(c)
        return carry

    lax.fori_loop(0, CAP, step, 0)


def base_kernel(tensors, early, down_hbm, up_hbm, x_ref, w_ref, *refs):
    block_refs, refs = refs[:early], refs[early:]
    keep_ref, send_ref, chosen_ref, up_ref, slot_ref, down_sems, up_sems = refs
    layers, _, depth = x_ref.shape
    width = keep_ref.shape[3]
    read_slots(block_refs, depth // HALVES, slot_ref)

    def copy_down(i, c):
        return fetch(down_hbm, slot_ref[i * CAP + c], chosen_ref.at[i], down_sems.at[i, c], c)

    def copy_up(i, c):
        return fetch(up_hbm, slot_ref[i * CAP + c], up_ref.at[i], up_sems.at[i, c], c)

    for copy in (copy_down, copy_up):
        for i in range(early):
            each_slot(lambda c, i=i, copy=copy: copy(i, c).start())
    me = lax.axis_index("tensor")
    for i, mask in enumerate(chunk_order(tensors)):
        out_ref = keep_ref if i < tensors // 2 else send_ref
        columns = pl.ds(pl.multiple_of((me ^ mask) * width, width), width)
        for layer in range(layers):
            out_ref[i % (tensors // 2), layer] = jnp.dot(
                x_ref[layer], w_ref[layer, :, columns], preferred_element_type=F32
            )
    for copy in (copy_down, copy_up):
        for i in range(early):
            each_slot(lambda c, i=i, copy=copy: copy(i, c).wait())


def down_kernel(early, down_hbm, up_hbm, early_ref, *refs):
    stores = len(refs) - 7
    block_refs, refs = refs[:stores], refs[stores:]
    low_ref, up_ref, late_ref, slot_ref, down_sems, up_sems, kept_ref = refs
    layers, _, rank, depth = down_hbm.shape
    half = depth // HALVES
    block = layers * HALVES * CAP
    late = stores - early
    read_slots(block_refs[early:], half, slot_ref)

    def copy_down(i, c):
        return fetch(down_hbm, slot_ref[i * CAP + c], late_ref.at[i], down_sems.at[i, c], c)

    def copy_up(i, c):
        return fetch(up_hbm, slot_ref[i * CAP + c], up_ref.at[i], up_sems.at[i, c], c)

    for copy in (copy_down, copy_up):
        for i in range(late):
            each_slot(lambda c, i=i, copy=copy: copy(i, c).start())
    row, column = iota((CAP * rank, block), 0), iota((CAP * rank, block), 1)
    for i in range(stores):
        chosen_ref = early_ref.at[i] if i < early else late_ref.at[i - early]
        if i >= early:
            each_slot(lambda c, i=i: copy_down(i - early, c).wait())
        total = jnp.zeros((rank, block), F32)
        for layer in range(layers):
            for part in range(HALVES):
                product = lax.dot_general(
                    chosen_ref[layer, :, part * half : (part + 1) * half],
                    block_refs[i][:, :half],
                    (((1,), (1,)), ((), ())),
                    preferred_element_type=F32,
                )
                mine = column == (layer * HALVES + part) * CAP + row // rank
                product = jnp.where(mine, product, 0.0)
                for c in range(CAP):
                    total = total + product[c * rank : (c + 1) * rank]
        kept_ref[:, i * block : (i + 1) * block] = total
    turned = kept_ref[...].T
    for i in range(stores):
        for layer in range(layers):
            at = i * block + layer * HALVES * CAP
            low_ref[(i * layers + layer) * CAP : (i * layers + layer + 1) * CAP] = (
                turned[at : at + CAP] + turned[at + CAP : at + 2 * CAP]
            )
    for i in range(late):
        each_slot(lambda c, i=i: copy_up(i, c).wait())


def pair_kernel(_, keep_ref, got_ref, own_ref, send_ref):
    own_ref[...] = keep_ref[0] + got_ref[0]
    send_ref[...] = keep_ref[1] + got_ref[1]


def up_kernel(tensors, _, early_ref, late_ref, *refs):
    low_refs, out_refs = refs[:tensors], refs[tensors:]
    early, layers, depth, width = early_ref.shape
    rank = depth // CAP
    half = width // HALVES
    low = low_refs[0][...]
    for low_ref in low_refs[1:]:
        low = low + low_ref[...]
    row, column = iota((CAP, depth), 0), iota((CAP, depth), 1)
    for i, out_ref in enumerate(out_refs):
        up_ref = early_ref.at[i] if i < early else late_ref.at[i - early]
        terms = []
        for layer in range(layers):
            at = (i * layers + layer) * CAP
            spread = jnp.concatenate([low[at : at + CAP]] * CAP, axis=1)
            spread = jnp.where(row == column // rank, spread, 0.0).astype(BF16)
            terms.append(jnp.dot(spread, up_ref[layer], preferred_element_type=F32))
        terms = jnp.concatenate(terms, axis=0)
        parts = [terms[:, part * half : (part + 1) * half] for part in range(HALVES)]
        out_ref[...] = jnp.concatenate(parts, axis=0).astype(BF16)


def final_kernel(count_ref, pick_ref, own_ref, got_ref, *refs):
    term_refs, out_ref = refs[:-1], refs[-1]
    layers, rows, width = out_ref.shape
    half = width // HALVES
    live = iota((rows, 1), 0) < count_ref[0]
    terms = [term_ref[...].astype(F32) for term_ref in term_refs]
    for part in range(HALVES):
        span = slice(part * half, (part + 1) * half)
        mine = slice(part * layers * CAP, (part + 1) * layers * CAP)
        stacked = jnp.concatenate([term[mine] for term in terms], axis=0).astype(BF16)
        delta = jnp.dot(pick_ref[...], stacked, preferred_element_type=F32)
        for layer in range(layers):
            total = own_ref[layer, :, span] + got_ref[layer, :, span]
            total = total + delta[layer * rows : (layer + 1) * rows]
            out_ref[layer, :, span] = jnp.where(live, total, 0.0).astype(BF16)


def params(limit=SMALL):
    return pltpu.CompilerParams(vmem_limit_bytes=limit)


def cost(microseconds):
    return pl.CostEstimate(
        flops=int(microseconds * 1.1535e9), bytes_accessed=0, transcendentals=0
    )


def local(stores, tensors, x, w, down, up, owner, slot, count):
    layers, rows, depth = x.shape
    adapters, rank, width = up.shape[1:]
    half = depth // HALVES
    block = layers * HALVES * CAP
    owner_row = owner.reshape(1, rows)
    slot_row = slot.reshape(1, rows)
    down = pltpu.with_memory_space_constraint(jnp.swapaxes(down, 2, 3), pltpu.HBM)
    up = pltpu.with_memory_space_constraint(up, pltpu.HBM)

    def swap(value, axis, size, by):
        if by == 0:
            return value
        return lax.ppermute(value, axis, [(i, i ^ by) for i in range(size)])

    order = [0] + list(range(stores // 2, stores)) + list(range(stores // 2 - 1, 0, -1))
    back = [0] + order[2:] + order[1:2]
    *payloads, pick = pl.pallas_call(
        functools.partial(prepare_kernel, back),
        out_shape=[jax.ShapeDtypeStruct((block, half + LANES), BF16)] * stores
        + [
            jax.ShapeDtypeStruct((layers * rows, stores * layers * CAP), BF16),
        ],
        in_specs=[ANY] * 3,
        out_specs=[VMEM] * (stores + 1),
        scratch_shapes=[
            pltpu.VMEM((1, rows), jnp.int32),
            pltpu.VMEM((1, rows), jnp.int32),
            pltpu.VMEM(x.shape, BF16),
            pltpu.SemaphoreType.DMA((3,)),
        ],
        compiler_params=params(),
        cost_estimate=cost(6),
        name="prepare",
    )(*(pltpu.with_memory_space_constraint(v, pltpu.HBM) for v in (owner_row, slot_row, x)))
    blocks = [swap(payloads[k], "store", stores, k) for k in order]

    early = min(2, stores)
    keep, send, chosen, early_up = pl.pallas_call(
        functools.partial(base_kernel, tensors, early),
        out_shape=[jax.ShapeDtypeStruct((tensors // 2, layers, rows, width), F32)] * 2
        + [
            jax.ShapeDtypeStruct((early, layers, CAP * rank, depth), BF16),
            jax.ShapeDtypeStruct((early, layers, CAP * rank, width), BF16),
        ],
        in_specs=[HBM] * 2 + [VMEM] * (2 + early),
        out_specs=[VMEM] * 4,
        scratch_shapes=[
            pltpu.SMEM((early * CAP,), jnp.int32),
            pltpu.SemaphoreType.DMA((early, CAP)),
            pltpu.SemaphoreType.DMA((early, CAP)),
        ],
        compiler_params=params(),
        cost_estimate=cost(6),
        name="base",
    )(down, up, x, w, *blocks[:early])

    late = stores - early
    low, late_up = pl.pallas_call(
        functools.partial(down_kernel, early),
        out_shape=[
            jax.ShapeDtypeStruct((stores * layers * CAP, rank), F32),
            jax.ShapeDtypeStruct((late, layers, CAP * rank, width), BF16),
        ],
        in_specs=[HBM] * 2 + [VMEM] * (1 + stores),
        out_specs=[VMEM] * 2,
        scratch_shapes=[
            pltpu.VMEM((late, layers, CAP * rank, depth), BF16),
            pltpu.SMEM((late * CAP,), jnp.int32),
            pltpu.SemaphoreType.DMA((late, CAP)),
            pltpu.SemaphoreType.DMA((late, CAP)),
            pltpu.VMEM((rank, stores * block), F32),
        ],
        compiler_params=params(LARGE),
        cost_estimate=cost(4),
        name="down",
    )(down, up, chosen, *blocks)
    lows = [low] + [swap(low, "tensor", tensors, j) for j in range(tensors - 1, 0, -1)]
    got = swap(send, "tensor", tensors, 1)
    bit = 2
    while keep.shape[0] > 2:
        total, middle = keep + got, keep.shape[0] // 2
        keep, got = total[:middle], swap(total[middle:], "tensor", tensors, bit)
        bit *= 2

    own, send = pl.pallas_call(
        pair_kernel,
        out_shape=[jax.ShapeDtypeStruct((layers, rows, width), F32)] * 2,
        in_specs=[ANY] + [VMEM] * 2,
        out_specs=[VMEM] * 2,
        compiler_params=params(),
        cost_estimate=cost(0.3),
        name="pair",
    )(low, keep, got)
    got = swap(send, "tensor", tensors, bit)

    terms = pl.pallas_call(
        functools.partial(up_kernel, tensors),
        out_shape=[jax.ShapeDtypeStruct((layers * HALVES * CAP, width // HALVES), BF16)] * stores,
        in_specs=[ANY] + [VMEM] * (2 + tensors),
        out_specs=[VMEM] * stores,
        compiler_params=params(),
        cost_estimate=cost(1),
        name="up",
    )(own, early_up, late_up, *lows)
    returned = [swap(terms[order.index(k)], "store", stores, k) for k in back]

    return pl.pallas_call(
        final_kernel,
        out_shape=jax.ShapeDtypeStruct((layers, rows, width), BF16),
        in_specs=[SMEM] + [VMEM] * (3 + stores),
        out_specs=VMEM,
        compiler_params=params(),
        cost_estimate=cost(1),
        name="final",
    )(count, pick, own, got, *returned)


def solution(mesh):
    return jax.shard_map(
        functools.partial(local, mesh.shape["store"], mesh.shape["tensor"]),
        mesh=mesh,
        in_specs=(
            P(None, ("groups", "store"), "tensor"),
            P(None, "tensor", None),
            P(None, "store", "tensor", None),
            P(None, "store", None, "tensor"),
            P(("groups", "store"), None),
            P(("groups", "store")),
            P(("groups", "store")),
        ),
        out_specs=P(None, ("groups", "store"), "tensor"),
        check_vma=False,
    )
```

```python
import functools

import jax
import jax.numpy as jnp
from jax import lax
from jax.experimental import pallas as pl
from jax.experimental.pallas import tpu as pltpu
from jax.sharding import PartitionSpec as P

CAP = 4
HALVES = 2
LANES = 128
F32 = jnp.float32
BF16 = jnp.bfloat16
VMEM = pl.BlockSpec(memory_space=pltpu.VMEM)
SMEM = pl.BlockSpec(memory_space=pltpu.SMEM)
HBM = pl.BlockSpec(memory_space=pltpu.HBM)
ANY = pl.BlockSpec(memory_space=pl.ANY)
SMALL = 8 * 1024 * 1024
LARGE = 24 * 1024 * 1024


def iota(shape, axis):
    return lax.broadcasted_iota(jnp.int32, shape, axis)


def ranks(owner_row):
    rows = owner_row.shape[1]
    down, across = iota((rows, rows), 0), iota((rows, rows), 1)
    owner_row = (owner_row ^ lax.axis_index("store")).astype(F32)
    spread = jnp.broadcast_to(owner_row, (rows, rows))
    owner_col = jnp.sum(jnp.where(down == across, spread, 0.0), axis=1, keepdims=True)
    same = owner_col == spread
    rank_row = jnp.sum(jnp.where(same & (down < across), 1.0, 0.0), axis=0, keepdims=True)
    rank_col = jnp.sum(jnp.where(same & (across < down), 1.0, 0.0), axis=1, keepdims=True)
    return owner_row, rank_row, owner_col, rank_col


def prepare_kernel(back, owner_hbm, slot_hbm, x_hbm, *refs):
    stores = len(back)
    out_refs, (pick_ref, owner_ref, slot_ref, x_ref, sems) = refs[:stores], refs[stores:]
    pairs = ((owner_hbm, owner_ref), (slot_hbm, slot_ref), (x_hbm, x_ref))
    copies = [
        pltpu.make_async_copy(source, target, sems.at[i]) for i, (source, target) in enumerate(pairs)
    ]
    for copy in copies:
        copy.start()
    for copy in copies[:2]:
        copy.wait()
    layers, rows, depth = x_ref.shape
    half = depth // HALVES
    block = layers * HALVES * CAP
    hop_row, rank_row, hop_col, rank_col = ranks(owner_ref[...])
    place = hop_row * block + rank_row
    places = jnp.concatenate([place + CAP * part for part in range(layers * HALVES)], axis=1)
    pick = iota((stores * block, layers * HALVES * rows), 0).astype(F32) == places
    spots = iota((rows, pick_ref.shape[1]), 1).astype(F32)
    spot = sum(jnp.where(hop_col == float(k), float(i), 0.0) for i, k in enumerate(back))
    back_place = spot * (layers * CAP) + rank_col
    for layer in range(layers):
        pick_ref[layer * rows : (layer + 1) * rows] = (spots == back_place + layer * CAP).astype(BF16)
    copies[2].wait()
    stacked = jnp.concatenate(
        [
            x_ref[layer, :, part * half : (part + 1) * half]
            for layer in range(layers)
            for part in range(HALVES)
        ],
        axis=0,
    )
    sent = jnp.dot(pick.astype(BF16), stacked, preferred_element_type=F32).astype(BF16)
    first = iota((stores * block, rows), 0).astype(F32) == place
    slots = jnp.sum(
        jnp.where(first, jnp.broadcast_to(slot_ref[...].astype(F32), first.shape), 0.0),
        axis=1,
        keepdims=True,
    )
    slots = jnp.broadcast_to(slots, (stores * block, LANES)).astype(BF16)
    for k, out_ref in enumerate(out_refs):
        out_ref[:, :half] = sent[k * block : (k + 1) * block]
        out_ref[:, half:] = slots[k * block : (k + 1) * block]


def chunk_order(tensors):
    if tensors == 1:
        return [0]
    rest = [2 * mask for mask in chunk_order(tensors // 2)]
    return rest + [mask + 1 for mask in rest]


def read_slots(block_refs, half, slot_ref):
    for i, block_ref in enumerate(block_refs):
        tail = block_ref[:, half:].astype(F32)
        for c in range(CAP):
            slot_ref[i * CAP + c] = tail[c, 0].astype(jnp.int32)


def fetch(store_hbm, slot, target_ref, sem, c):
    rank = store_hbm.shape[2]
    return pltpu.make_async_copy(
        store_hbm.at[:, slot], target_ref.at[:, pl.ds(pl.multiple_of(c * rank, rank), rank)], sem
    )


def each_slot(body):
    def step(c, carry):
        body(c)
        return carry

    lax.fori_loop(0, CAP, step, 0)


def multiply_layer(layer, x_ref, w_ref, keep_ref, send_ref):
    half = keep_ref.shape[0]
    width = keep_ref.shape[-1]
    me = lax.axis_index("tensor")
    for i, mask in enumerate(chunk_order(2 * half)):
        out_ref = keep_ref if i < half else send_ref
        columns = pl.ds(pl.multiple_of((me ^ mask) * width, width), width)
        out_ref[i % half, layer] = jnp.dot(
            x_ref[layer], w_ref[layer, :, columns], preferred_element_type=F32
        )


def both_copies(down_hbm, up_hbm, slot_ref, chosen_ref, up_ref, down_sems, up_sems):
    def copy_down(i, c):
        return fetch(down_hbm, slot_ref[i * CAP + c], chosen_ref.at[i], down_sems.at[i, c], c)

    def copy_up(i, c):
        return fetch(up_hbm, slot_ref[i * CAP + c], up_ref.at[i], up_sems.at[i, c], c)

    return copy_down, copy_up


def early_kernel(down_hbm, up_hbm, x_ref, w_ref, block_ref, *refs):
    keep_ref, send_ref, chosen_ref, up_ref, slot_ref, down_sems, up_sems = refs
    read_slots([block_ref], x_ref.shape[2] // HALVES, slot_ref)
    copies = both_copies(down_hbm, up_hbm, slot_ref, chosen_ref, up_ref, down_sems, up_sems)
    for copy in copies:
        each_slot(lambda c, copy=copy: copy(0, c).start())
    multiply_layer(0, x_ref, w_ref, keep_ref, send_ref)
    for copy in copies:
        each_slot(lambda c, copy=copy: copy(0, c).wait())


def late_kernel(down_hbm, up_hbm, x_ref, w_ref, keep0_ref, send0_ref, early_ref, *refs):
    stores = len(refs) - 9
    block_refs, refs = refs[:stores], refs[stores:]
    keep_ref, send_ref, low_ref, up_ref, late_ref, slot_ref, down_sems, up_sems, kept_ref = refs
    layers, _, rank, depth = down_hbm.shape
    half = depth // HALVES
    block = layers * HALVES * CAP
    read_slots(block_refs[1:], half, slot_ref)
    copy_down, copy_up = both_copies(
        down_hbm, up_hbm, slot_ref, late_ref, up_ref, down_sems, up_sems
    )
    for copy in (copy_down, copy_up):
        for i in range(stores - 1):
            each_slot(lambda c, i=i, copy=copy: copy(i, c).start())
    keep_ref[:, 0] = keep0_ref[:, 0]
    send_ref[:, 0] = send0_ref[:, 0]
    for layer in range(1, layers):
        multiply_layer(layer, x_ref, w_ref, keep_ref, send_ref)
    row, column = iota((CAP * rank, block), 0), iota((CAP * rank, block), 1)
    for i in range(stores):
        chosen_ref = early_ref.at[0] if i == 0 else late_ref.at[i - 1]
        if i > 0:
            each_slot(lambda c, i=i: copy_down(i - 1, c).wait())
        total = jnp.zeros((rank, block), F32)
        for layer in range(layers):
            for part in range(HALVES):
                product = lax.dot_general(
                    chosen_ref[layer, :, part * half : (part + 1) * half],
                    block_refs[i][:, :half],
                    (((1,), (1,)), ((), ())),
                    preferred_element_type=F32,
                )
                mine = column == (layer * HALVES + part) * CAP + row // rank
                product = jnp.where(mine, product, 0.0)
                for c in range(CAP):
                    total = total + product[c * rank : (c + 1) * rank]
        kept_ref[:, i * block : (i + 1) * block] = total
    turned = kept_ref[...].T
    for i in range(stores):
        for layer in range(layers):
            at = i * block + layer * HALVES * CAP
            low_ref[(i * layers + layer) * CAP : (i * layers + layer + 1) * CAP] = (
                turned[at : at + CAP] + turned[at + CAP : at + 2 * CAP]
            )
    for i in range(stores - 1):
        each_slot(lambda c, i=i: copy_up(i, c).wait())


def pair_kernel(_, keep_ref, got_ref, own_ref, send_ref):
    own_ref[...] = keep_ref[0] + got_ref[0]
    send_ref[...] = keep_ref[1] + got_ref[1]


def up_kernel(tensors, _, early_ref, late_ref, *refs):
    low_refs, out_refs = refs[:tensors], refs[tensors:]
    early, layers, depth, width = early_ref.shape
    rank = depth // CAP
    half = width // HALVES
    low = low_refs[0][...]
    for low_ref in low_refs[1:]:
        low = low + low_ref[...]
    row, column = iota((CAP, depth), 0), iota((CAP, depth), 1)
    for i, out_ref in enumerate(out_refs):
        up_ref = early_ref.at[i] if i < early else late_ref.at[i - early]
        terms = []
        for layer in range(layers):
            at = (i * layers + layer) * CAP
            spread = jnp.concatenate([low[at : at + CAP]] * CAP, axis=1)
            spread = jnp.where(row == column // rank, spread, 0.0).astype(BF16)
            terms.append(jnp.dot(spread, up_ref[layer], preferred_element_type=F32))
        terms = jnp.concatenate(terms, axis=0)
        parts = [terms[:, part * half : (part + 1) * half] for part in range(HALVES)]
        out_ref[...] = jnp.concatenate(parts, axis=0).astype(BF16)


def final_kernel(count_ref, pick_ref, own_ref, got_ref, *refs):
    term_refs, out_ref = refs[:-1], refs[-1]
    layers, rows, width = out_ref.shape
    half = width // HALVES
    live = iota((rows, 1), 0) < count_ref[0]
    terms = [term_ref[...].astype(F32) for term_ref in term_refs]
    for part in range(HALVES):
        span = slice(part * half, (part + 1) * half)
        mine = slice(part * layers * CAP, (part + 1) * layers * CAP)
        stacked = jnp.concatenate([term[mine] for term in terms], axis=0).astype(BF16)
        delta = jnp.dot(pick_ref[...], stacked, preferred_element_type=F32)
        for layer in range(layers):
            total = own_ref[layer, :, span] + got_ref[layer, :, span]
            total = total + delta[layer * rows : (layer + 1) * rows]
            out_ref[layer, :, span] = jnp.where(live, total, 0.0).astype(BF16)


def params(limit=SMALL):
    return pltpu.CompilerParams(vmem_limit_bytes=limit)


def cost(microseconds):
    return pl.CostEstimate(
        flops=int(microseconds * 1.1535e9), bytes_accessed=0, transcendentals=0
    )


def local(stores, tensors, x, w, down, up, owner, slot, count):
    layers, rows, depth = x.shape
    adapters, rank, width = up.shape[1:]
    half = depth // HALVES
    block = layers * HALVES * CAP
    owner_row = owner.reshape(1, rows)
    slot_row = slot.reshape(1, rows)
    down = pltpu.with_memory_space_constraint(jnp.swapaxes(down, 2, 3), pltpu.HBM)
    up = pltpu.with_memory_space_constraint(up, pltpu.HBM)

    def swap(value, axis, size, by):
        if by == 0:
            return value
        return lax.ppermute(value, axis, [(i, i ^ by) for i in range(size)])

    order = [0] + list(range(stores // 2, stores)) + list(range(stores // 2 - 1, 0, -1))
    back = [0] + order[2:] + order[1:2]
    *payloads, pick = pl.pallas_call(
        functools.partial(prepare_kernel, back),
        out_shape=[jax.ShapeDtypeStruct((block, half + LANES), BF16)] * stores
        + [
            jax.ShapeDtypeStruct((layers * rows, stores * layers * CAP), BF16),
        ],
        in_specs=[ANY] * 3,
        out_specs=[VMEM] * (stores + 1),
        scratch_shapes=[
            pltpu.VMEM((1, rows), jnp.int32),
            pltpu.VMEM((1, rows), jnp.int32),
            pltpu.VMEM(x.shape, BF16),
            pltpu.SemaphoreType.DMA((3,)),
        ],
        compiler_params=params(),
        cost_estimate=cost(6),
        name="prepare",
    )(*(pltpu.with_memory_space_constraint(v, pltpu.HBM) for v in (owner_row, slot_row, x)))
    blocks = [swap(payloads[k], "store", stores, k) for k in order]

    def sums(some_layers):
        return [jax.ShapeDtypeStruct((tensors // 2, some_layers, rows, width), F32)] * 2

    keep, send, chosen, early_up = pl.pallas_call(
        early_kernel,
        out_shape=sums(1)
        + [
            jax.ShapeDtypeStruct((1, layers, CAP * rank, depth), BF16),
            jax.ShapeDtypeStruct((1, layers, CAP * rank, width), BF16),
        ],
        in_specs=[HBM] * 2 + [VMEM] * 3,
        out_specs=[VMEM] * 4,
        scratch_shapes=[
            pltpu.SMEM((CAP,), jnp.int32),
            pltpu.SemaphoreType.DMA((1, CAP)),
            pltpu.SemaphoreType.DMA((1, CAP)),
        ],
        compiler_params=params(),
        cost_estimate=cost(3),
        name="early",
    )(down, up, x, w, blocks[0])

    late = stores - 1
    keep, send, low, late_up = pl.pallas_call(
        late_kernel,
        out_shape=sums(layers)
        + [
            jax.ShapeDtypeStruct((stores * layers * CAP, rank), F32),
            jax.ShapeDtypeStruct((late, layers, CAP * rank, width), BF16),
        ],
        in_specs=[HBM] * 2 + [VMEM] * (5 + stores),
        out_specs=[VMEM] * 4,
        scratch_shapes=[
            pltpu.VMEM((late, layers, CAP * rank, depth), BF16),
            pltpu.SMEM((late * CAP,), jnp.int32),
            pltpu.SemaphoreType.DMA((late, CAP)),
            pltpu.SemaphoreType.DMA((late, CAP)),
            pltpu.VMEM((rank, stores * block), F32),
        ],
        compiler_params=params(LARGE),
        cost_estimate=cost(6),
        name="late",
    )(down, up, x, w, keep, send, chosen, *blocks)
    lows = [low] + [swap(low, "tensor", tensors, j) for j in range(tensors - 1, 0, -1)]
    got = swap(send, "tensor", tensors, 1)
    bit = 2
    while keep.shape[0] > 2:
        total, middle = keep + got, keep.shape[0] // 2
        keep, got = total[:middle], swap(total[middle:], "tensor", tensors, bit)
        bit *= 2

    own, send = pl.pallas_call(
        pair_kernel,
        out_shape=[jax.ShapeDtypeStruct((layers, rows, width), F32)] * 2,
        in_specs=[ANY] + [VMEM] * 2,
        out_specs=[VMEM] * 2,
        compiler_params=params(),
        cost_estimate=cost(0.3),
        name="pair",
    )(low, keep, got)
    got = swap(send, "tensor", tensors, bit)

    terms = pl.pallas_call(
        functools.partial(up_kernel, tensors),
        out_shape=[jax.ShapeDtypeStruct((layers * HALVES * CAP, width // HALVES), BF16)] * stores,
        in_specs=[ANY] + [VMEM] * (2 + tensors),
        out_specs=[VMEM] * stores,
        compiler_params=params(),
        cost_estimate=cost(1),
        name="up",
    )(own, early_up, late_up, *lows)
    returned = [swap(terms[order.index(k)], "store", stores, k) for k in back]

    return pl.pallas_call(
        final_kernel,
        out_shape=jax.ShapeDtypeStruct((layers, rows, width), BF16),
        in_specs=[SMEM] + [VMEM] * (3 + stores),
        out_specs=VMEM,
        compiler_params=params(),
        cost_estimate=cost(1),
        name="final",
    )(count, pick, own, got, *returned)


def solution(mesh):
    return jax.shard_map(
        functools.partial(local, mesh.shape["store"], mesh.shape["tensor"]),
        mesh=mesh,
        in_specs=(
            P(None, ("groups", "store"), "tensor"),
            P(None, "tensor", None),
            P(None, "store", "tensor", None),
            P(None, "store", None, "tensor"),
            P(("groups", "store"), None),
            P(("groups", "store")),
            P(("groups", "store")),
        ),
        out_specs=P(None, ("groups", "store"), "tensor"),
        check_vma=False,
    )
```

```python
import functools

import jax
import jax.numpy as jnp
from jax import lax
from jax.experimental import pallas as pl
from jax.experimental.pallas import tpu as pltpu
from jax.sharding import PartitionSpec as P

CAP = 4
HALVES = 2
LANES = 128
F32 = jnp.float32
BF16 = jnp.bfloat16
VMEM = pl.BlockSpec(memory_space=pltpu.VMEM)
SMEM = pl.BlockSpec(memory_space=pltpu.SMEM)
HBM = pl.BlockSpec(memory_space=pltpu.HBM)
ANY = pl.BlockSpec(memory_space=pl.ANY)
SMALL = 8 * 1024 * 1024
LARGE = 24 * 1024 * 1024


def iota(shape, axis):
    return lax.broadcasted_iota(jnp.int32, shape, axis)


def ranks(owner_row):
    rows = owner_row.shape[1]
    down, across = iota((rows, rows), 0), iota((rows, rows), 1)
    owner_row = (owner_row ^ lax.axis_index("store")).astype(F32)
    spread = jnp.broadcast_to(owner_row, (rows, rows))
    owner_col = jnp.sum(jnp.where(down == across, spread, 0.0), axis=1, keepdims=True)
    same = owner_col == spread
    rank_row = jnp.sum(jnp.where(same & (down < across), 1.0, 0.0), axis=0, keepdims=True)
    rank_col = jnp.sum(jnp.where(same & (across < down), 1.0, 0.0), axis=1, keepdims=True)
    return owner_row, rank_row, owner_col, rank_col


def prepare_kernel(back, owner_hbm, slot_hbm, x_hbm, *refs):
    stores = len(back)
    out_refs, (pick_ref, owner_ref, slot_ref, x_ref, sems) = refs[:stores], refs[stores:]
    pairs = ((owner_hbm, owner_ref), (slot_hbm, slot_ref), (x_hbm, x_ref))
    copies = [
        pltpu.make_async_copy(source, target, sems.at[i]) for i, (source, target) in enumerate(pairs)
    ]
    for copy in copies:
        copy.start()
    for copy in copies[:2]:
        copy.wait()
    layers, rows, depth = x_ref.shape
    half = depth // HALVES
    block = layers * HALVES * CAP
    hop_row, rank_row, hop_col, rank_col = ranks(owner_ref[...])
    place = hop_row * block + rank_row
    places = jnp.concatenate([place + CAP * part for part in range(layers * HALVES)], axis=1)
    pick = iota((stores * block, layers * HALVES * rows), 0).astype(F32) == places
    spots = iota((rows, pick_ref.shape[1]), 1).astype(F32)
    spot = sum(jnp.where(hop_col == float(k), float(i), 0.0) for i, k in enumerate(back))
    back_place = spot * (layers * CAP) + rank_col
    for layer in range(layers):
        pick_ref[layer * rows : (layer + 1) * rows] = (spots == back_place + layer * CAP).astype(BF16)
    copies[2].wait()
    stacked = jnp.concatenate(
        [
            x_ref[layer, :, part * half : (part + 1) * half]
            for layer in range(layers)
            for part in range(HALVES)
        ],
        axis=0,
    )
    sent = jnp.dot(pick.astype(BF16), stacked, preferred_element_type=F32).astype(BF16)
    first = iota((stores * block, rows), 0).astype(F32) == place
    slots = jnp.sum(
        jnp.where(first, jnp.broadcast_to(slot_ref[...].astype(F32), first.shape), 0.0),
        axis=1,
        keepdims=True,
    )
    slots = jnp.broadcast_to(slots, (stores * block, LANES)).astype(BF16)
    for k, out_ref in enumerate(out_refs):
        out_ref[:, :half] = sent[k * block : (k + 1) * block]
        out_ref[:, half:] = slots[k * block : (k + 1) * block]


def chunk_order(tensors):
    if tensors == 1:
        return [0]
    rest = [2 * mask for mask in chunk_order(tensors // 2)]
    return rest + [mask + 1 for mask in rest]


def read_slots(block_refs, half, slot_ref):
    for i, block_ref in enumerate(block_refs):
        tail = block_ref[:, half:].astype(F32)
        for c in range(CAP):
            slot_ref[i * CAP + c] = tail[c, 0].astype(jnp.int32)


def fetch(store_hbm, slot, target_ref, sem, c):
    rank = store_hbm.shape[2]
    return pltpu.make_async_copy(
        store_hbm.at[:, slot], target_ref.at[:, pl.ds(pl.multiple_of(c * rank, rank), rank)], sem
    )


def each_slot(body):
    def step(c, carry):
        body(c)
        return carry

    lax.fori_loop(0, CAP, step, 0)


def base_kernel(tensors, early, down_hbm, up_hbm, x_ref, w_ref, *refs):
    block_refs, refs = refs[:early], refs[early:]
    keep_ref, send_ref, chosen_ref, up_ref, slot_ref, down_sems, up_sems = refs
    layers, _, depth = x_ref.shape
    width = keep_ref.shape[3]
    read_slots(block_refs, depth // HALVES, slot_ref)

    def copy_down(i, c):
        return fetch(down_hbm, slot_ref[i * CAP + c], chosen_ref.at[i], down_sems.at[i, c], c)

    def copy_up(i, c):
        return fetch(up_hbm, slot_ref[i * CAP + c], up_ref.at[i], up_sems.at[i, c], c)

    for copy in (copy_down, copy_up):
        for i in range(early):
            each_slot(lambda c, i=i, copy=copy: copy(i, c).start())
    me = lax.axis_index("tensor")
    for i, mask in enumerate(chunk_order(tensors)):
        out_ref = keep_ref if i < tensors // 2 else send_ref
        columns = pl.ds(pl.multiple_of((me ^ mask) * width, width), width)
        for layer in range(layers):
            out_ref[i % (tensors // 2), layer] = jnp.dot(
                x_ref[layer], w_ref[layer, :, columns], preferred_element_type=F32
            )
    for copy in (copy_down, copy_up):
        for i in range(early):
            each_slot(lambda c, i=i, copy=copy: copy(i, c).wait())


def down_kernel(early, down_hbm, up_hbm, early_ref, *refs):
    stores = len(refs) - 7
    block_refs, refs = refs[:stores], refs[stores:]
    low_ref, up_ref, late_ref, slot_ref, down_sems, up_sems, kept_ref = refs
    layers, _, rank, depth = down_hbm.shape
    half = depth // HALVES
    block = layers * HALVES * CAP
    late = stores - early
    read_slots(block_refs[early:], half, slot_ref)

    def copy_down(i, c):
        return fetch(down_hbm, slot_ref[i * CAP + c], late_ref.at[i], down_sems.at[i, c], c)

    def copy_up(i, c):
        return fetch(up_hbm, slot_ref[i * CAP + c], up_ref.at[i], up_sems.at[i, c], c)

    for copy in (copy_down, copy_up):
        for i in range(late):
            each_slot(lambda c, i=i, copy=copy: copy(i, c).start())
    row, column = iota((CAP * rank, block), 0), iota((CAP * rank, block), 1)
    for i in range(stores):
        chosen_ref = early_ref.at[i] if i < early else late_ref.at[i - early]
        if i >= early:
            each_slot(lambda c, i=i: copy_down(i - early, c).wait())
        total = jnp.zeros((rank, block), F32)
        for layer in range(layers):
            for part in range(HALVES):
                product = lax.dot_general(
                    chosen_ref[layer, :, part * half : (part + 1) * half],
                    block_refs[i][:, :half],
                    (((1,), (1,)), ((), ())),
                    preferred_element_type=F32,
                )
                mine = column == (layer * HALVES + part) * CAP + row // rank
                product = jnp.where(mine, product, 0.0)
                for c in range(CAP):
                    total = total + product[c * rank : (c + 1) * rank]
        kept_ref[:, i * block : (i + 1) * block] = total
    turned = kept_ref[...].T
    for i in range(stores):
        for layer in range(layers):
            at = i * block + layer * HALVES * CAP
            low_ref[(i * layers + layer) * CAP : (i * layers + layer + 1) * CAP] = (
                turned[at : at + CAP] + turned[at + CAP : at + 2 * CAP]
            )
    for i in range(late):
        each_slot(lambda c, i=i: copy_up(i, c).wait())


def pair_kernel(_, keep_ref, got_ref, own_ref, send_ref):
    own_ref[...] = keep_ref[0] + got_ref[0]
    send_ref[...] = keep_ref[1] + got_ref[1]


def up_kernel(tensors, _, early_ref, late_ref, *refs):
    low_refs, out_refs = refs[:tensors], refs[tensors:]
    early, layers, depth, width = early_ref.shape
    rank = depth // CAP
    half = width // HALVES
    low = low_refs[0][...]
    for low_ref in low_refs[1:]:
        low = low + low_ref[...]
    row, column = iota((CAP, depth), 0), iota((CAP, depth), 1)
    for i, out_ref in enumerate(out_refs):
        up_ref = early_ref.at[i] if i < early else late_ref.at[i - early]
        terms = []
        for layer in range(layers):
            at = (i * layers + layer) * CAP
            spread = jnp.concatenate([low[at : at + CAP]] * CAP, axis=1)
            spread = jnp.where(row == column // rank, spread, 0.0).astype(BF16)
            terms.append(jnp.dot(spread, up_ref[layer], preferred_element_type=F32))
        terms = jnp.concatenate(terms, axis=0)
        parts = [terms[:, part * half : (part + 1) * half] for part in range(HALVES)]
        out_ref[...] = jnp.concatenate(parts, axis=0).astype(BF16)


def final_kernel(count_ref, pick_ref, own_ref, got_ref, *refs):
    term_refs, out_ref = refs[:-1], refs[-1]
    layers, rows, width = out_ref.shape
    half = width // HALVES
    live = iota((rows, 1), 0) < count_ref[0]
    terms = [term_ref[...].astype(F32) for term_ref in term_refs]
    for part in range(HALVES):
        span = slice(part * half, (part + 1) * half)
        mine = slice(part * layers * CAP, (part + 1) * layers * CAP)
        stacked = jnp.concatenate([term[mine] for term in terms], axis=0).astype(BF16)
        delta = jnp.dot(pick_ref[...], stacked, preferred_element_type=F32)
        for layer in range(layers):
            total = own_ref[layer, :, span] + got_ref[layer, :, span]
            total = total + delta[layer * rows : (layer + 1) * rows]
            out_ref[layer, :, span] = jnp.where(live, total, 0.0).astype(BF16)


def params(limit=SMALL):
    return pltpu.CompilerParams(vmem_limit_bytes=limit)


def cost(microseconds):
    return pl.CostEstimate(
        flops=int(microseconds * 1.1535e9), bytes_accessed=0, transcendentals=0
    )


def local(stores, tensors, x, w, down, up, owner, slot, count):
    layers, rows, depth = x.shape
    adapters, rank, width = up.shape[1:]
    half = depth // HALVES
    block = layers * HALVES * CAP
    owner_row = owner.reshape(1, rows)
    slot_row = slot.reshape(1, rows)
    down = pltpu.with_memory_space_constraint(jnp.swapaxes(down, 2, 3), pltpu.HBM)
    up = pltpu.with_memory_space_constraint(up, pltpu.HBM)

    def swap(value, axis, size, by):
        if by == 0:
            return value
        return lax.ppermute(value, axis, [(i, i ^ by) for i in range(size)])

    order = [0] + list(range(stores // 2, stores)) + list(range(stores // 2 - 1, 0, -1))
    back = [0] + order[2:] + order[1:2]
    *payloads, pick = pl.pallas_call(
        functools.partial(prepare_kernel, back),
        out_shape=[jax.ShapeDtypeStruct((block, half + LANES), BF16)] * stores
        + [
            jax.ShapeDtypeStruct((layers * rows, stores * layers * CAP), BF16),
        ],
        in_specs=[ANY] * 3,
        out_specs=[VMEM] * (stores + 1),
        scratch_shapes=[
            pltpu.VMEM((1, rows), jnp.int32),
            pltpu.VMEM((1, rows), jnp.int32),
            pltpu.VMEM(x.shape, BF16),
            pltpu.SemaphoreType.DMA((3,)),
        ],
        compiler_params=params(),
        cost_estimate=cost(6),
        name="prepare",
    )(*(pltpu.with_memory_space_constraint(v, pltpu.HBM) for v in (owner_row, slot_row, x)))
    blocks = [swap(payloads[k], "store", stores, k) for k in order]

    early = 1
    keep, send, chosen, early_up = pl.pallas_call(
        functools.partial(base_kernel, tensors, early),
        out_shape=[jax.ShapeDtypeStruct((tensors // 2, layers, rows, width), F32)] * 2
        + [
            jax.ShapeDtypeStruct((early, layers, CAP * rank, depth), BF16),
            jax.ShapeDtypeStruct((early, layers, CAP * rank, width), BF16),
        ],
        in_specs=[HBM] * 2 + [VMEM] * (2 + early),
        out_specs=[VMEM] * 4,
        scratch_shapes=[
            pltpu.SMEM((early * CAP,), jnp.int32),
            pltpu.SemaphoreType.DMA((early, CAP)),
            pltpu.SemaphoreType.DMA((early, CAP)),
        ],
        compiler_params=params(),
        cost_estimate=cost(6),
        name="base",
    )(down, up, x, w, *blocks[:early])

    late = stores - early
    low, late_up = pl.pallas_call(
        functools.partial(down_kernel, early),
        out_shape=[
            jax.ShapeDtypeStruct((stores * layers * CAP, rank), F32),
            jax.ShapeDtypeStruct((late, layers, CAP * rank, width), BF16),
        ],
        in_specs=[HBM] * 2 + [VMEM] * (1 + stores),
        out_specs=[VMEM] * 2,
        scratch_shapes=[
            pltpu.VMEM((late, layers, CAP * rank, depth), BF16),
            pltpu.SMEM((late * CAP,), jnp.int32),
            pltpu.SemaphoreType.DMA((late, CAP)),
            pltpu.SemaphoreType.DMA((late, CAP)),
            pltpu.VMEM((rank, stores * block), F32),
        ],
        compiler_params=params(LARGE),
        cost_estimate=cost(4),
        name="down",
    )(down, up, chosen, *blocks)
    lows = [low] + [swap(low, "tensor", tensors, j) for j in range(tensors - 1, 0, -1)]
    got = swap(send, "tensor", tensors, 1)
    bit = 2
    while keep.shape[0] > 2:
        total, middle = keep + got, keep.shape[0] // 2
        keep, got = total[:middle], swap(total[middle:], "tensor", tensors, bit)
        bit *= 2

    own, send = pl.pallas_call(
        pair_kernel,
        out_shape=[jax.ShapeDtypeStruct((layers, rows, width), F32)] * 2,
        in_specs=[ANY] + [VMEM] * 2,
        out_specs=[VMEM] * 2,
        compiler_params=params(),
        cost_estimate=cost(0.3),
        name="pair",
    )(low, keep, got)
    got = swap(send, "tensor", tensors, bit)

    terms = pl.pallas_call(
        functools.partial(up_kernel, tensors),
        out_shape=[jax.ShapeDtypeStruct((layers * HALVES * CAP, width // HALVES), BF16)] * stores,
        in_specs=[ANY] + [VMEM] * (2 + tensors),
        out_specs=[VMEM] * stores,
        compiler_params=params(),
        cost_estimate=cost(1),
        name="up",
    )(own, early_up, late_up, *lows)
    returned = [swap(terms[order.index(k)], "store", stores, k) for k in back]

    return pl.pallas_call(
        final_kernel,
        out_shape=jax.ShapeDtypeStruct((layers, rows, width), BF16),
        in_specs=[SMEM] + [VMEM] * (3 + stores),
        out_specs=VMEM,
        compiler_params=params(),
        cost_estimate=cost(1),
        name="final",
    )(count, pick, own, got, *returned)


def solution(mesh):
    return jax.shard_map(
        functools.partial(local, mesh.shape["store"], mesh.shape["tensor"]),
        mesh=mesh,
        in_specs=(
            P(None, ("groups", "store"), "tensor"),
            P(None, "tensor", None),
            P(None, "store", "tensor", None),
            P(None, "store", None, "tensor"),
            P(("groups", "store"), None),
            P(("groups", "store")),
            P(("groups", "store")),
        ),
        out_specs=P(None, ("groups", "store"), "tensor"),
        check_vma=False,
    )
```

```python
import functools

import jax
import jax.numpy as jnp
from jax import lax
from jax.experimental import pallas as pl
from jax.experimental.pallas import tpu as pltpu
from jax.sharding import PartitionSpec as P

CAP = 4
FIRST, LAST = -1, -2
HALVES = 2
LANES = 128
F32 = jnp.float32
BF16 = jnp.bfloat16
VMEM = pl.BlockSpec(memory_space=pltpu.VMEM)
SMEM = pl.BlockSpec(memory_space=pltpu.SMEM)
HBM = pl.BlockSpec(memory_space=pltpu.HBM)
ANY = pl.BlockSpec(memory_space=pl.ANY)
SMALL = 8 * 1024 * 1024
LARGE = 24 * 1024 * 1024


def iota(shape, axis):
    return lax.broadcasted_iota(jnp.int32, shape, axis)


def ranks(owner_row):
    rows = owner_row.shape[1]
    down, across = iota((rows, rows), 0), iota((rows, rows), 1)
    owner_row = (owner_row ^ lax.axis_index("store")).astype(F32)
    spread = jnp.broadcast_to(owner_row, (rows, rows))
    owner_col = jnp.sum(jnp.where(down == across, spread, 0.0), axis=1, keepdims=True)
    same = owner_col == spread
    rank_row = jnp.sum(jnp.where(same & (down < across), 1.0, 0.0), axis=0, keepdims=True)
    rank_col = jnp.sum(jnp.where(same & (across < down), 1.0, 0.0), axis=1, keepdims=True)
    return owner_row, rank_row, owner_col, rank_col


def prepare_kernel(back, owner_hbm, slot_hbm, x_hbm, *refs):
    stores = len(back)
    out_refs, (pick_ref, owner_ref, slot_ref, x_ref, sems) = refs[:stores], refs[stores:]
    pairs = ((owner_hbm, owner_ref), (slot_hbm, slot_ref), (x_hbm, x_ref))
    copies = [
        pltpu.make_async_copy(source, target, sems.at[i]) for i, (source, target) in enumerate(pairs)
    ]
    for copy in copies:
        copy.start()
    for copy in copies[:2]:
        copy.wait()
    layers, rows, depth = x_ref.shape
    half = depth // HALVES
    block = layers * HALVES * CAP
    hop_row, rank_row, hop_col, rank_col = ranks(owner_ref[...])
    place = hop_row * block + rank_row
    places = jnp.concatenate([place + CAP * part for part in range(layers * HALVES)], axis=1)
    pick = iota((stores * block, layers * HALVES * rows), 0).astype(F32) == places
    spots = iota((rows, pick_ref.shape[1]), 1).astype(F32)
    spot = sum(jnp.where(hop_col == float(k), float(i), 0.0) for i, k in enumerate(back))
    back_place = spot * (layers * CAP) + rank_col
    for layer in range(layers):
        pick_ref[layer * rows : (layer + 1) * rows] = (spots == back_place + layer * CAP).astype(BF16)
    copies[2].wait()
    stacked = jnp.concatenate(
        [
            x_ref[layer, :, part * half : (part + 1) * half]
            for layer in range(layers)
            for part in range(HALVES)
        ],
        axis=0,
    )
    sent = jnp.dot(pick.astype(BF16), stacked, preferred_element_type=F32).astype(BF16)
    first = iota((stores * block, rows), 0).astype(F32) == place
    slots = jnp.sum(
        jnp.where(first, jnp.broadcast_to(slot_ref[...].astype(F32), first.shape), 0.0),
        axis=1,
        keepdims=True,
    )
    slots = jnp.broadcast_to(slots, (stores * block, LANES)).astype(BF16)
    for k, out_ref in enumerate(out_refs):
        out_ref[:, :half] = sent[k * block : (k + 1) * block]
        out_ref[:, half:] = slots[k * block : (k + 1) * block]


def chunk_order(tensors):
    if tensors == 1:
        return [0]
    rest = [2 * mask for mask in chunk_order(tensors // 2)]
    return rest + [mask + 1 for mask in rest]


def read_slots(block_refs, half, slot_ref):
    for i, block_ref in enumerate(block_refs):
        tail = block_ref[:, half:].astype(F32)
        for c in range(CAP):
            slot_ref[i * CAP + c] = tail[c, 0].astype(jnp.int32)


def fetch(store_hbm, slot, target_ref, sem, c):
    rank = store_hbm.shape[2]
    return pltpu.make_async_copy(
        store_hbm.at[:, slot], target_ref.at[:, pl.ds(pl.multiple_of(c * rank, rank), rank)], sem
    )


def each_slot(body):
    def step(c, carry):
        body(c)
        return carry

    lax.fori_loop(0, CAP, step, 0)


def base_kernel(tensors, early, down_hbm, up_hbm, x_ref, w_ref, *refs):
    block_refs, refs = refs[:early], refs[early:]
    keep_ref, send_ref, chosen_ref, up_ref, slot_ref, down_sems, up_sems = refs
    layers, _, depth = x_ref.shape
    width = keep_ref.shape[3]
    read_slots(block_refs, depth // HALVES, slot_ref)

    def copy_down(i, c):
        return fetch(down_hbm, slot_ref[i * CAP + c], chosen_ref.at[i], down_sems.at[i, c], c)

    def copy_up(i, c):
        return fetch(up_hbm, slot_ref[i * CAP + c], up_ref.at[i], up_sems.at[i, c], c)

    for copy in (copy_down, copy_up):
        for i in range(early):
            each_slot(lambda c, i=i, copy=copy: copy(i, c).start())
    me = lax.axis_index("tensor")
    for i, mask in enumerate(chunk_order(tensors)):
        out_ref = keep_ref if i < tensors // 2 else send_ref
        columns = pl.ds(pl.multiple_of((me ^ mask) * width, width), width)
        for layer in range(layers):
            out_ref[i % (tensors // 2), layer] = jnp.dot(
                x_ref[layer], w_ref[layer, :, columns], preferred_element_type=F32
            )
    for copy in (copy_down, copy_up):
        for i in range(early):
            each_slot(lambda c, i=i, copy=copy: copy(i, c).wait())


def down_kernel(early, down_hbm, up_hbm, early_ref, *refs):
    stores = len(refs) - 7
    block_refs, refs = refs[:stores], refs[stores:]
    low_ref, up_ref, late_ref, slot_ref, down_sems, up_sems, kept_ref = refs
    layers, _, rank, depth = down_hbm.shape
    half = depth // HALVES
    block = layers * HALVES * CAP
    late = stores - early
    read_slots(block_refs[early:], half, slot_ref)

    def copy_down(i, c):
        return fetch(down_hbm, slot_ref[i * CAP + c], late_ref.at[i], down_sems.at[i, c], c)

    def copy_up(i, c):
        return fetch(up_hbm, slot_ref[i * CAP + c], up_ref.at[i], up_sems.at[i, c], c)

    for copy in (copy_down, copy_up):
        for i in range(late):
            each_slot(lambda c, i=i, copy=copy: copy(i, c).start())
    row, column = iota((CAP * rank, block), 0), iota((CAP * rank, block), 1)
    for i in range(stores):
        chosen_ref = early_ref.at[i] if i < early else late_ref.at[i - early]
        if i >= early:
            each_slot(lambda c, i=i: copy_down(i - early, c).wait())
        total = jnp.zeros((rank, block), F32)
        for layer in range(layers):
            for part in range(HALVES):
                product = lax.dot_general(
                    chosen_ref[layer, :, part * half : (part + 1) * half],
                    block_refs[i][:, :half],
                    (((1,), (1,)), ((), ())),
                    preferred_element_type=F32,
                )
                mine = column == (layer * HALVES + part) * CAP + row // rank
                product = jnp.where(mine, product, 0.0)
                for c in range(CAP):
                    total = total + product[c * rank : (c + 1) * rank]
        kept_ref[:, i * block : (i + 1) * block] = total
    turned = kept_ref[...].T
    for i in range(stores):
        for layer in range(layers):
            at = i * block + layer * HALVES * CAP
            low_ref[(i * layers + layer) * CAP : (i * layers + layer + 1) * CAP] = (
                turned[at : at + CAP] + turned[at + CAP : at + 2 * CAP]
            )
    for i in range(late):
        each_slot(lambda c, i=i: copy_up(i, c).wait())


def pair_kernel(_, keep_ref, got_ref, own_ref, send_ref):
    own_ref[...] = keep_ref[0] + got_ref[0]
    send_ref[...] = keep_ref[1] + got_ref[1]


def up_kernel(tensors, _, early_ref, late_ref, *refs):
    low_refs, out_refs = refs[:tensors], refs[tensors:]
    early, layers, depth, width = early_ref.shape
    rank = depth // CAP
    half = width // HALVES
    low = low_refs[0][...]
    for low_ref in low_refs[1:]:
        low = low + low_ref[...]
    row, column = iota((CAP, depth), 0), iota((CAP, depth), 1)
    for i, out_ref in enumerate(out_refs):
        up_ref = early_ref.at[i] if i < early else late_ref.at[i - early]
        terms = []
        for layer in range(layers):
            at = (i * layers + layer) * CAP
            spread = jnp.concatenate([low[at : at + CAP]] * CAP, axis=1)
            spread = jnp.where(row == column // rank, spread, 0.0).astype(BF16)
            terms.append(jnp.dot(spread, up_ref[layer], preferred_element_type=F32))
        terms = jnp.concatenate(terms, axis=0)
        parts = [terms[:, part * half : (part + 1) * half] for part in range(HALVES)]
        out_ref[...] = jnp.concatenate(parts, axis=0).astype(BF16)


def final_kernel(lanes, count_ref, pick_ref, own_ref, got_ref, *refs):
    term_refs, out_ref = refs[:-1], refs[-1]
    layers, rows, width = out_ref.shape
    half = width // HALVES
    live = iota((rows, 1), 0) < count_ref[0]
    named = {k: term_ref[...].astype(F32) for k, term_ref in zip([0, *lanes], term_refs)}
    terms = [named[k] for k in range(len(lanes) - 1)] + [named[FIRST] + named[LAST]]
    for part in range(HALVES):
        span = slice(part * half, (part + 1) * half)
        mine = slice(part * layers * CAP, (part + 1) * layers * CAP)
        stacked = jnp.concatenate([term[mine] for term in terms], axis=0).astype(BF16)
        delta = jnp.dot(pick_ref[...], stacked, preferred_element_type=F32)
        for layer in range(layers):
            total = own_ref[layer, :, span] + got_ref[layer, :, span]
            total = total + delta[layer * rows : (layer + 1) * rows]
            out_ref[layer, :, span] = jnp.where(live, total, 0.0).astype(BF16)


def params(limit=SMALL):
    return pltpu.CompilerParams(vmem_limit_bytes=limit)


def cost(microseconds):
    return pl.CostEstimate(
        flops=int(microseconds * 1.1535e9), bytes_accessed=0, transcendentals=0
    )


def local(stores, tensors, x, w, down, up, owner, slot, count):
    layers, rows, depth = x.shape
    adapters, rank, width = up.shape[1:]
    half = depth // HALVES
    block = layers * HALVES * CAP
    owner_row = owner.reshape(1, rows)
    slot_row = slot.reshape(1, rows)
    down = pltpu.with_memory_space_constraint(jnp.swapaxes(down, 2, 3), pltpu.HBM)
    up = pltpu.with_memory_space_constraint(up, pltpu.HBM)

    def swap(value, axis, size, by):
        if by == 0:
            return value
        return lax.ppermute(value, axis, [(i, i ^ by) for i in range(size)])

    order = [0] + list(range(stores // 2, stores)) + list(range(stores // 2 - 1, 0, -1))
    far = stores - 1

    def spread_back(values):
        pairs = [(i, i ^ far) for i in range(stores)]
        chosen = {FIRST: pairs[-1:], LAST: pairs[:-1]}
        return [
            lax.ppermute(values[far], "store", chosen[k])
            if k in chosen
            else swap(values[k], "store", stores, k)
            for k in back_lanes
        ]

    back_lanes = [LAST, FIRST] + list(range(1, far))
    *payloads, pick = pl.pallas_call(
        functools.partial(prepare_kernel, list(range(stores))),
        out_shape=[jax.ShapeDtypeStruct((block, half + LANES), BF16)] * stores
        + [
            jax.ShapeDtypeStruct((layers * rows, stores * layers * CAP), BF16),
        ],
        in_specs=[ANY] * 3,
        out_specs=[VMEM] * (stores + 1),
        scratch_shapes=[
            pltpu.VMEM((1, rows), jnp.int32),
            pltpu.VMEM((1, rows), jnp.int32),
            pltpu.VMEM(x.shape, BF16),
            pltpu.SemaphoreType.DMA((3,)),
        ],
        compiler_params=params(),
        cost_estimate=cost(6),
        name="prepare",
    )(*(pltpu.with_memory_space_constraint(v, pltpu.HBM) for v in (owner_row, slot_row, x)))
    blocks = [swap(payloads[k], "store", stores, k) for k in order]

    early = 1
    keep, send, chosen, early_up = pl.pallas_call(
        functools.partial(base_kernel, tensors, early),
        out_shape=[jax.ShapeDtypeStruct((tensors // 2, layers, rows, width), F32)] * 2
        + [
            jax.ShapeDtypeStruct((early, layers, CAP * rank, depth), BF16),
            jax.ShapeDtypeStruct((early, layers, CAP * rank, width), BF16),
        ],
        in_specs=[HBM] * 2 + [VMEM] * (2 + early),
        out_specs=[VMEM] * 4,
        scratch_shapes=[
            pltpu.SMEM((early * CAP,), jnp.int32),
            pltpu.SemaphoreType.DMA((early, CAP)),
            pltpu.SemaphoreType.DMA((early, CAP)),
        ],
        compiler_params=params(),
        cost_estimate=cost(6),
        name="base",
    )(down, up, x, w, *blocks[:early])

    late = stores - early
    low, late_up = pl.pallas_call(
        functools.partial(down_kernel, early),
        out_shape=[
            jax.ShapeDtypeStruct((stores * layers * CAP, rank), F32),
            jax.ShapeDtypeStruct((late, layers, CAP * rank, width), BF16),
        ],
        in_specs=[HBM] * 2 + [VMEM] * (1 + stores),
        out_specs=[VMEM] * 2,
        scratch_shapes=[
            pltpu.VMEM((late, layers, CAP * rank, depth), BF16),
            pltpu.SMEM((late * CAP,), jnp.int32),
            pltpu.SemaphoreType.DMA((late, CAP)),
            pltpu.SemaphoreType.DMA((late, CAP)),
            pltpu.VMEM((rank, stores * block), F32),
        ],
        compiler_params=params(LARGE),
        cost_estimate=cost(4),
        name="down",
    )(down, up, chosen, *blocks)
    lows = [low] + [swap(low, "tensor", tensors, j) for j in range(tensors - 1, 0, -1)]
    got = swap(send, "tensor", tensors, 1)
    bit = 2
    while keep.shape[0] > 2:
        total, middle = keep + got, keep.shape[0] // 2
        keep, got = total[:middle], swap(total[middle:], "tensor", tensors, bit)
        bit *= 2

    own, send = pl.pallas_call(
        pair_kernel,
        out_shape=[jax.ShapeDtypeStruct((layers, rows, width), F32)] * 2,
        in_specs=[ANY] + [VMEM] * 2,
        out_specs=[VMEM] * 2,
        compiler_params=params(),
        cost_estimate=cost(0.3),
        name="pair",
    )(low, keep, got)
    got = swap(send, "tensor", tensors, bit)

    terms = pl.pallas_call(
        functools.partial(up_kernel, tensors),
        out_shape=[jax.ShapeDtypeStruct((layers * HALVES * CAP, width // HALVES), BF16)] * stores,
        in_specs=[ANY] + [VMEM] * (2 + tensors),
        out_specs=[VMEM] * stores,
        compiler_params=params(),
        cost_estimate=cost(1),
        name="up",
    )(own, early_up, late_up, *lows)
    terms = {k: term for k, term in zip(order, terms)}
    returned = [terms[0], *spread_back(terms)]

    return pl.pallas_call(
        functools.partial(final_kernel, back_lanes),
        out_shape=jax.ShapeDtypeStruct((layers, rows, width), BF16),
        in_specs=[SMEM] + [VMEM] * (4 + stores),
        out_specs=VMEM,
        compiler_params=params(),
        cost_estimate=cost(1),
        name="final",
    )(count, pick, own, got, *returned)


def solution(mesh):
    return jax.shard_map(
        functools.partial(local, mesh.shape["store"], mesh.shape["tensor"]),
        mesh=mesh,
        in_specs=(
            P(None, ("groups", "store"), "tensor"),
            P(None, "tensor", None),
            P(None, "store", "tensor", None),
            P(None, "store", None, "tensor"),
            P(("groups", "store"), None),
            P(("groups", "store")),
            P(("groups", "store")),
        ),
        out_specs=P(None, ("groups", "store"), "tensor"),
        check_vma=False,
    )
```

```python
import functools

import jax
import jax.numpy as jnp
from jax import lax
from jax.experimental import pallas as pl
from jax.experimental.pallas import tpu as pltpu
from jax.sharding import PartitionSpec as P

CAP = 4
HALVES = 2
LANES = 128
F32 = jnp.float32
BF16 = jnp.bfloat16
VMEM = pl.BlockSpec(memory_space=pltpu.VMEM)
SMEM = pl.BlockSpec(memory_space=pltpu.SMEM)
HBM = pl.BlockSpec(memory_space=pltpu.HBM)
ANY = pl.BlockSpec(memory_space=pl.ANY)
SMALL = 8 * 1024 * 1024
LARGE = 24 * 1024 * 1024


def iota(shape, axis):
    return lax.broadcasted_iota(jnp.int32, shape, axis)


def ranks(owner_row):
    rows = owner_row.shape[1]
    down, across = iota((rows, rows), 0), iota((rows, rows), 1)
    owner_row = (owner_row ^ lax.axis_index("store")).astype(F32)
    spread = jnp.broadcast_to(owner_row, (rows, rows))
    owner_col = jnp.sum(jnp.where(down == across, spread, 0.0), axis=1, keepdims=True)
    same = owner_col == spread
    rank_row = jnp.sum(jnp.where(same & (down < across), 1.0, 0.0), axis=0, keepdims=True)
    rank_col = jnp.sum(jnp.where(same & (across < down), 1.0, 0.0), axis=1, keepdims=True)
    return owner_row, rank_row, owner_col, rank_col


def prepare_kernel(back, owner_hbm, slot_hbm, x_hbm, *refs):
    stores = len(back)
    out_refs, (pick_ref, owner_ref, slot_ref, x_ref, sems) = refs[:stores], refs[stores:]
    pairs = ((owner_hbm, owner_ref), (slot_hbm, slot_ref), (x_hbm, x_ref))
    copies = [
        pltpu.make_async_copy(source, target, sems.at[i]) for i, (source, target) in enumerate(pairs)
    ]
    for copy in copies:
        copy.start()
    for copy in copies[:2]:
        copy.wait()
    layers, rows, depth = x_ref.shape
    half = depth // HALVES
    block = layers * HALVES * CAP
    hop_row, rank_row, hop_col, rank_col = ranks(owner_ref[...])
    place = hop_row * block + rank_row
    places = jnp.concatenate([place + CAP * part for part in range(layers * HALVES)], axis=1)
    pick = iota((stores * block, layers * HALVES * rows), 0).astype(F32) == places
    spots = iota((rows, pick_ref.shape[1]), 1).astype(F32)
    spot = sum(jnp.where(hop_col == float(k), float(i), 0.0) for i, k in enumerate(back))
    back_place = spot * (layers * CAP) + rank_col
    for layer in range(layers):
        pick_ref[layer * rows : (layer + 1) * rows] = (spots == back_place + layer * CAP).astype(BF16)
    copies[2].wait()
    stacked = jnp.concatenate(
        [
            x_ref[layer, :, part * half : (part + 1) * half]
            for layer in range(layers)
            for part in range(HALVES)
        ],
        axis=0,
    )
    sent = jnp.dot(pick.astype(BF16), stacked, preferred_element_type=F32).astype(BF16)
    first = iota((stores * block, rows), 0).astype(F32) == place
    slots = jnp.sum(
        jnp.where(first, jnp.broadcast_to(slot_ref[...].astype(F32), first.shape), 0.0),
        axis=1,
        keepdims=True,
    )
    slots = jnp.broadcast_to(slots, (stores * block, LANES)).astype(BF16)
    for k, out_ref in enumerate(out_refs):
        out_ref[:, :half] = sent[k * block : (k + 1) * block]
        out_ref[:, half:] = slots[k * block : (k + 1) * block]


def chunk_order(tensors):
    if tensors == 1:
        return [0]
    rest = [2 * mask for mask in chunk_order(tensors // 2)]
    return rest + [mask + 1 for mask in rest]


def read_slots(block_refs, half, slot_ref):
    for i, block_ref in enumerate(block_refs):
        tail = block_ref[:, half:].astype(F32)
        for c in range(CAP):
            slot_ref[i * CAP + c] = tail[c, 0].astype(jnp.int32)


def fetch(store_hbm, slot, target_ref, sem, c):
    rank = store_hbm.shape[2]
    return pltpu.make_async_copy(
        store_hbm.at[:, slot], target_ref.at[:, pl.ds(pl.multiple_of(c * rank, rank), rank)], sem
    )


def each_slot(body):
    def step(c, carry):
        body(c)
        return carry

    lax.fori_loop(0, CAP, step, 0)


def base_kernel(tensors, early, down_hbm, up_hbm, x_ref, w_ref, *refs):
    block_refs, refs = refs[:early], refs[early:]
    keep_ref, send_ref, chosen_ref, up_ref, slot_ref, down_sems, up_sems = refs
    layers, _, depth = x_ref.shape
    width = keep_ref.shape[3]
    read_slots(block_refs, depth // HALVES, slot_ref)

    def copy_down(i, c):
        return fetch(down_hbm, slot_ref[i * CAP + c], chosen_ref.at[i], down_sems.at[i, c], c)

    def copy_up(i, c):
        return fetch(up_hbm, slot_ref[i * CAP + c], up_ref.at[i], up_sems.at[i, c], c)

    for copy in (copy_down, copy_up):
        for i in range(early):
            each_slot(lambda c, i=i, copy=copy: copy(i, c).start())
    me = lax.axis_index("tensor")
    for i, mask in enumerate(chunk_order(tensors)):
        out_ref = keep_ref if i < tensors // 2 else send_ref
        columns = pl.ds(pl.multiple_of((me ^ mask) * width, width), width)
        for layer in range(layers):
            out_ref[i % (tensors // 2), layer] = jnp.dot(
                x_ref[layer], w_ref[layer, :, columns], preferred_element_type=F32
            )
    for copy in (copy_down, copy_up):
        for i in range(early):
            each_slot(lambda c, i=i, copy=copy: copy(i, c).wait())


def down_kernel(early, down_hbm, up_hbm, early_ref, *refs):
    stores = len(refs) - 7
    block_refs, refs = refs[:stores], refs[stores:]
    low_ref, up_ref, late_ref, slot_ref, down_sems, up_sems, kept_ref = refs
    layers, _, rank, depth = down_hbm.shape
    half = depth // HALVES
    block = layers * HALVES * CAP
    late = stores - early
    read_slots(block_refs[early:], half, slot_ref)

    def copy_down(i, layer, c):
        return pltpu.make_async_copy(
            down_hbm.at[layer, slot_ref[i * CAP + c]],
            late_ref.at[i, layer, pl.ds(pl.multiple_of(c * rank, rank), rank)],
            down_sems.at[i, layer, c],
        )

    def copy_up(i, c):
        return fetch(up_hbm, slot_ref[i * CAP + c], up_ref.at[i], up_sems.at[i, c], c)

    for i in range(late):
        for layer in range(layers):
            each_slot(lambda c, i=i, layer=layer: copy_down(i, layer, c).start())
    for i in range(late):
        each_slot(lambda c, i=i: copy_up(i, c).start())
    row, column = iota((CAP * rank, block), 0), iota((CAP * rank, block), 1)
    for i in range(stores):
        chosen_ref = early_ref.at[i] if i < early else late_ref.at[i - early]
        total = jnp.zeros((rank, block), F32)
        for layer in range(layers):
            if i >= early:
                each_slot(lambda c, i=i, layer=layer: copy_down(i - early, layer, c).wait())
            for part in range(HALVES):
                product = lax.dot_general(
                    chosen_ref[layer, :, part * half : (part + 1) * half],
                    block_refs[i][:, :half],
                    (((1,), (1,)), ((), ())),
                    preferred_element_type=F32,
                )
                mine = column == (layer * HALVES + part) * CAP + row // rank
                product = jnp.where(mine, product, 0.0)
                for c in range(CAP):
                    total = total + product[c * rank : (c + 1) * rank]
        kept_ref[:, i * block : (i + 1) * block] = total
    turned = kept_ref[...].T
    for i in range(stores):
        for layer in range(layers):
            at = i * block + layer * HALVES * CAP
            low_ref[(i * layers + layer) * CAP : (i * layers + layer + 1) * CAP] = (
                turned[at : at + CAP] + turned[at + CAP : at + 2 * CAP]
            )
    for i in range(late):
        each_slot(lambda c, i=i: copy_up(i, c).wait())


def pair_kernel(_, keep_ref, got_ref, own_ref, send_ref):
    own_ref[...] = keep_ref[0] + got_ref[0]
    send_ref[...] = keep_ref[1] + got_ref[1]


def up_kernel(tensors, _, early_ref, late_ref, *refs):
    low_refs, out_refs = refs[:tensors], refs[tensors:]
    early, layers, depth, width = early_ref.shape
    rank = depth // CAP
    half = width // HALVES
    low = low_refs[0][...]
    for low_ref in low_refs[1:]:
        low = low + low_ref[...]
    row, column = iota((CAP, depth), 0), iota((CAP, depth), 1)
    for i, out_ref in enumerate(out_refs):
        up_ref = early_ref.at[i] if i < early else late_ref.at[i - early]
        terms = []
        for layer in range(layers):
            at = (i * layers + layer) * CAP
            spread = jnp.concatenate([low[at : at + CAP]] * CAP, axis=1)
            spread = jnp.where(row == column // rank, spread, 0.0).astype(BF16)
            terms.append(jnp.dot(spread, up_ref[layer], preferred_element_type=F32))
        terms = jnp.concatenate(terms, axis=0)
        parts = [terms[:, part * half : (part + 1) * half] for part in range(HALVES)]
        out_ref[...] = jnp.concatenate(parts, axis=0).astype(BF16)


def final_kernel(count_ref, pick_ref, own_ref, got_ref, *refs):
    term_refs, out_ref = refs[:-1], refs[-1]
    layers, rows, width = out_ref.shape
    half = width // HALVES
    live = iota((rows, 1), 0) < count_ref[0]
    terms = [term_ref[...].astype(F32) for term_ref in term_refs]
    for part in range(HALVES):
        span = slice(part * half, (part + 1) * half)
        mine = slice(part * layers * CAP, (part + 1) * layers * CAP)
        stacked = jnp.concatenate([term[mine] for term in terms], axis=0).astype(BF16)
        delta = jnp.dot(pick_ref[...], stacked, preferred_element_type=F32)
        for layer in range(layers):
            total = own_ref[layer, :, span] + got_ref[layer, :, span]
            total = total + delta[layer * rows : (layer + 1) * rows]
            out_ref[layer, :, span] = jnp.where(live, total, 0.0).astype(BF16)


def params(limit=SMALL):
    return pltpu.CompilerParams(vmem_limit_bytes=limit)


def cost(microseconds):
    return pl.CostEstimate(
        flops=int(microseconds * 1.1535e9), bytes_accessed=0, transcendentals=0
    )


def local(stores, tensors, x, w, down, up, owner, slot, count):
    layers, rows, depth = x.shape
    adapters, rank, width = up.shape[1:]
    half = depth // HALVES
    block = layers * HALVES * CAP
    owner_row = owner.reshape(1, rows)
    slot_row = slot.reshape(1, rows)
    down = pltpu.with_memory_space_constraint(jnp.swapaxes(down, 2, 3), pltpu.HBM)
    up = pltpu.with_memory_space_constraint(up, pltpu.HBM)

    def swap(value, axis, size, by):
        if by == 0:
            return value
        return lax.ppermute(value, axis, [(i, i ^ by) for i in range(size)])

    order = [0] + list(range(stores // 2, stores)) + list(range(stores // 2 - 1, 0, -1))
    back = [0] + order[2:] + order[1:2]
    *payloads, pick = pl.pallas_call(
        functools.partial(prepare_kernel, back),
        out_shape=[jax.ShapeDtypeStruct((block, half + LANES), BF16)] * stores
        + [
            jax.ShapeDtypeStruct((layers * rows, stores * layers * CAP), BF16),
        ],
        in_specs=[ANY] * 3,
        out_specs=[VMEM] * (stores + 1),
        scratch_shapes=[
            pltpu.VMEM((1, rows), jnp.int32),
            pltpu.VMEM((1, rows), jnp.int32),
            pltpu.VMEM(x.shape, BF16),
            pltpu.SemaphoreType.DMA((3,)),
        ],
        compiler_params=params(),
        cost_estimate=cost(6),
        name="prepare",
    )(*(pltpu.with_memory_space_constraint(v, pltpu.HBM) for v in (owner_row, slot_row, x)))
    blocks = [swap(payloads[k], "store", stores, k) for k in order]

    early = 1
    keep, send, chosen, early_up = pl.pallas_call(
        functools.partial(base_kernel, tensors, early),
        out_shape=[jax.ShapeDtypeStruct((tensors // 2, layers, rows, width), F32)] * 2
        + [
            jax.ShapeDtypeStruct((early, layers, CAP * rank, depth), BF16),
            jax.ShapeDtypeStruct((early, layers, CAP * rank, width), BF16),
        ],
        in_specs=[HBM] * 2 + [VMEM] * (2 + early),
        out_specs=[VMEM] * 4,
        scratch_shapes=[
            pltpu.SMEM((early * CAP,), jnp.int32),
            pltpu.SemaphoreType.DMA((early, CAP)),
            pltpu.SemaphoreType.DMA((early, CAP)),
        ],
        compiler_params=params(),
        cost_estimate=cost(6),
        name="base",
    )(down, up, x, w, *blocks[:early])

    late = stores - early
    low, late_up = pl.pallas_call(
        functools.partial(down_kernel, early),
        out_shape=[
            jax.ShapeDtypeStruct((stores * layers * CAP, rank), F32),
            jax.ShapeDtypeStruct((late, layers, CAP * rank, width), BF16),
        ],
        in_specs=[HBM] * 2 + [VMEM] * (1 + stores),
        out_specs=[VMEM] * 2,
        scratch_shapes=[
            pltpu.VMEM((late, layers, CAP * rank, depth), BF16),
            pltpu.SMEM((late * CAP,), jnp.int32),
            pltpu.SemaphoreType.DMA((late, layers, CAP)),
            pltpu.SemaphoreType.DMA((late, CAP)),
            pltpu.VMEM((rank, stores * block), F32),
        ],
        compiler_params=params(LARGE),
        cost_estimate=cost(4),
        name="down",
    )(down, up, chosen, *blocks)
    lows = [low] + [swap(low, "tensor", tensors, j) for j in range(tensors - 1, 0, -1)]
    got = swap(send, "tensor", tensors, 1)
    bit = 2
    while keep.shape[0] > 2:
        total, middle = keep + got, keep.shape[0] // 2
        keep, got = total[:middle], swap(total[middle:], "tensor", tensors, bit)
        bit *= 2

    own, send = pl.pallas_call(
        pair_kernel,
        out_shape=[jax.ShapeDtypeStruct((layers, rows, width), F32)] * 2,
        in_specs=[ANY] + [VMEM] * 2,
        out_specs=[VMEM] * 2,
        compiler_params=params(),
        cost_estimate=cost(0.3),
        name="pair",
    )(low, keep, got)
    got = swap(send, "tensor", tensors, bit)

    terms = pl.pallas_call(
        functools.partial(up_kernel, tensors),
        out_shape=[jax.ShapeDtypeStruct((layers * HALVES * CAP, width // HALVES), BF16)] * stores,
        in_specs=[ANY] + [VMEM] * (2 + tensors),
        out_specs=[VMEM] * stores,
        compiler_params=params(),
        cost_estimate=cost(1),
        name="up",
    )(own, early_up, late_up, *lows)
    returned = [swap(terms[order.index(k)], "store", stores, k) for k in back]

    return pl.pallas_call(
        final_kernel,
        out_shape=jax.ShapeDtypeStruct((layers, rows, width), BF16),
        in_specs=[SMEM] + [VMEM] * (3 + stores),
        out_specs=VMEM,
        compiler_params=params(),
        cost_estimate=cost(1),
        name="final",
    )(count, pick, own, got, *returned)


def solution(mesh):
    return jax.shard_map(
        functools.partial(local, mesh.shape["store"], mesh.shape["tensor"]),
        mesh=mesh,
        in_specs=(
            P(None, ("groups", "store"), "tensor"),
            P(None, "tensor", None),
            P(None, "store", "tensor", None),
            P(None, "store", None, "tensor"),
            P(("groups", "store"), None),
            P(("groups", "store")),
            P(("groups", "store")),
        ),
        out_specs=P(None, ("groups", "store"), "tensor"),
        check_vma=False,
    )
```
